128 devices in a mesh: row: 4 (over x), rad: 32 (over y, z, core).
Axes of the slice: x: 4, y: 4, z: 4, core: 2. Of those that a mesh axis runs over, the one named last changes fastest.
Arguments:
- adjoint_cells: float32 [4, 256, 17, 5, 512], P('row', 'rad'), may hold values from -6 to 6
- flux_jacobian: bfloat16 [4, 256, 17, 5, 5, 512], P('row', 'rad'), may hold values from -2 to 2
- dissipation: float32 [4, 256, 512], P('row', 'rad'), may hold values from 0.2 to 2
- face_rows: float32 [2048, 17, 5, 128], P(('row', 'rad')), may hold values from -6 to 6
- owners: int32 [2048, 17, 3], P(('row', 'rad')), may hold values from 0 to 511, all different within a row; in each aligned block of 272 rows (0 to 271, 272 to 543, ..., all dimensions but the last counted through in order) at most 2 rows name the same one
- margin_weights: float32 [2048, 17, 3], P(('row', 'rad')), may hold values from 0.25 to 1
- transposed_maps: bfloat16 [512, 128, 128], P(('row', 'rad')), may hold values from -0.5 to 0.5
Outputs:
- cell_gradient: float32 [4, 256, 17, 5, 512], P('row', 'rad')
- face_gradient: float32 [2048, 17, 5, 128], P(('row', 'rad'))
The draws below stay inside these ranges and needn't reach their ends.
Inputs may be any that keep to these rules, and one draw needn't show every extreme that they name: `owners`: each row names 3 different stator blocks; among the rows of one device's face tiles no block is named more than 2 times, and some block exactly 2 times.
All inputs are finite; a program needn't handle non-finite values.
Results may differ from the reference program's by a relative error of at most 0.002.
Values may be sent and summed in bfloat16 or wider, within the bound.
No kernel may reach another device: no remote copies, remote signals or barrier semaphores. Data moves between devices by JAX's collectives and lax.ppermute only.
A program may use at most 64 MiB of HBM per device.

```python
import math
import jax
import jax.numpy as jnp
import numpy as np
from jax import lax

NT = 17
NH = 5
F = 5
FACE = 128
K = 3
NP = 512
FT_DEV = 16
PB = 4
NR = 256
FT = 2048
SB = 512
CAP = 2


def steps_of(key, extent, shards, smallest, largest):
    gain = 1.0
    for dim, shards_of in shards:
        steps = jax.random.uniform(jax.random.fold_in(jax.random.fold_in(key, 6), dim), (shards_of,), jnp.float32, smallest / len(shards), largest / len(shards))
        gain = gain * jnp.repeat(jnp.exp(steps), extent[dim] // shards_of).reshape((-1,) + (1,) * (len(extent) - 1 - dim))
    return gain


def routed_block(rng, own, number, rows, number_of, top, reach, slope):
    order = jax.random.permutation(rng, number_of)
    packed, common = shares(number_of, rows * top, reach, slope, True), shares(number_of, rows * top, reach, slope, False)
    places = jnp.arange(number_of)

    def named(sizes, offset_by):
        used = int((sizes > 0).sum())
        fixed = max(1, used // 4)
        passed = fixed + (places - fixed + offset_by * (used - fixed)) % max(1, number_of - fixed)
        return jnp.zeros((number_of,), jnp.int32).at[order[jnp.where(places < fixed, places, passed)]].set(jnp.asarray(sizes, jnp.int32))

    sizes = jnp.where(number % 4 == 0, named(packed, number // 4), named(common, number - number // 4 - 1))
    mixed = jax.random.permutation(jax.random.fold_in(own, 3), number_of)
    giver, receiver = mixed[0:number_of // 2 * 2:2], mixed[1:number_of // 2 * 2:2]
    room = jnp.minimum(sizes[giver] - 1, reach - sizes[receiver]) // 2
    room = jnp.where((giver == order[0]) | (receiver == order[0]) | (sizes[receiver] == 0), 0, jnp.maximum(room, 0))
    passed = jax.random.randint(jax.random.fold_in(own, 4), (number_of // 2,), 0, 1 << 20) % (room + 1)
    sizes = sizes.at[giver].add(-passed).at[receiver].add(passed)
    labels = jnp.searchsorted(jnp.cumsum(sizes), jnp.arange(rows * top), side="right").astype(jnp.int32)
    listing = labels.reshape(top, rows).T
    listing = listing[jax.random.permutation(jax.random.fold_in(own, 1), rows)]
    offset_by = jax.random.randint(jax.random.fold_in(own, 2), (rows, 1), 0, top)
    return jnp.take_along_axis(listing, (jnp.arange(top)[None, :] + offset_by) % top, axis=1)


def shares(number_of, total, most, slope, full):
    portions = [(1 << 20) // math.isqrt(grade ** slope) + 1 for grade in range(1, number_of + 1)]
    largest = most if full else min(most, max(-(-total // number_of), total * portions[0] // sum(portions)))
    least = 1 if total - largest >= number_of - 1 else 0
    given, spare = [largest] + [least] * (number_of - 1), total - largest - least * (number_of - 1)
    while spare > 0:
        candidates = [i for i in range(1, number_of) if given[i] < largest] or [i for i in range(1, number_of) if given[i] < most]
        mass, remaining = sum([portions[i] for i in candidates]), spare
        for i in candidates:
            addition = min(most - given[i], max(1, remaining * portions[i] // mass), spare)
            given[i] = given[i] + addition
            spare = spare - addition
    return np.array(given)


def scatter_about(key, dims, scale, most, cuts=(), kind=jnp.bfloat16):
    factor_of = steps_of(key, dims, cuts, -0.22, 0.18) if cuts else 1.0
    values = jax.random.normal(key, dims, jnp.float32) * scale * factor_of
    return jnp.minimum(jnp.maximum(values, -most), most).astype(kind)


def setup_inputs(seed: int = 0) -> dict:
    key_of = jax.random.split(jax.random.key(seed), 8)
    adjoint_cells = scatter_about(key_of[0], (PB, NR, NT, F, NP), 1.0, 6.0, ((0, 4), (1, 32)), jnp.float32)
    flux_jacobian = scatter_about(key_of[1], (PB, NR, NT, F, F, NP), 0.3, 2.0, ((0, 4), (1, 32)))
    dissipation = jnp.clip(jnp.exp(math.log(2.0) - 2.3025851 * jax.random.uniform(key_of[2], (PB, NR, NP), jnp.float32) ** steps_of(key_of[2], (PB, NR, NP), ((0, 4), (1, 32)), -0.2, 0.2)), 0.2, 2.0)
    face_rows = scatter_about(key_of[3], (FT, NT, F, FACE), 1.0, 6.0, ((0, 128),), jnp.float32)
    owners_keys = jax.random.split(jax.random.fold_in(key_of[4], 1), FT * NT // (FT_DEV * NT))
    owners_turns = jax.random.permutation(jax.random.fold_in(key_of[4], 3), FT * NT // (FT_DEV * NT))
    owners = jax.vmap(lambda own, number: routed_block(jax.random.fold_in(key_of[4], 2), own, number, FT_DEV * NT, SB, K, CAP, 2))(owners_keys, owners_turns).reshape((FT, NT, K))
    margin_weights = jnp.clip(0.25 + 0.75 * jax.random.uniform(key_of[5], (FT, NT, K), jnp.float32) ** steps_of(key_of[5], (FT, NT, K), ((0, 128),), -0.2, 0.2), 0.25, 1.0)
    transposed_maps = scatter_about(key_of[6], (SB, FACE, FACE), FACE ** -0.5, 0.5, ((0, 128),))
    return {"adjoint_cells": adjoint_cells, "flux_jacobian": flux_jacobian, "dissipation": dissipation, "face_rows": face_rows, "owners": owners, "margin_weights": margin_weights, "transposed_maps": transposed_maps}


def derivative_matrix():
    instance = jnp.arange(NT)
    offset = (instance[:, None] - instance[None, :]).astype(jnp.float32)
    harmonic = jnp.arange(1, NH + 1).astype(jnp.float32)
    angles = 2.0 * math.pi * harmonic * offset[..., None] / NT
    return -(2.0 * 0.5 / NT) * jnp.sum(harmonic * jnp.sin(angles), axis=-1)


def time_adjoint(field):
    derivative = derivative_matrix()
    flat = field.reshape((-1,) + field.shape[-3:])
    result = jnp.einsum("st,asfn->atfn", derivative, flat, precision=lax.Precision.HIGHEST)
    return result.reshape(field.shape)


def reference(adjoint_cells, flux_jacobian, dissipation, face_rows, owners, margin_weights, transposed_maps):
    time_cells = time_adjoint(adjoint_cells)
    jac_term = jnp.sum(flux_jacobian.astype(jnp.float32) * adjoint_cells[..., :, None, :], axis=-3)
    weighted_field = dissipation[:, :, None, None, :] * adjoint_cells
    padded = jnp.pad(weighted_field, ((0, 0), (1, 1), (0, 0), (0, 0), (0, 0)))
    laplace = padded[:, 2:] - 2.0 * weighted_field + padded[:, :-2]
    cell_gradient = time_cells + jac_term - laplace

    rounded_rows = face_rows.astype(jnp.bfloat16)

    def tile_group(inputs):
        group_rows, group_owners, group_weights = inputs
        group_maps = transposed_maps[group_owners].astype(jnp.float32)
        partial_value = jnp.einsum("atfi,atkij->atkfj", group_rows.astype(jnp.float32), group_maps)
        return jnp.sum(group_weights[..., None, None] * partial_value, axis=2)

    grouped = (rounded_rows.reshape((-1, FT_DEV, NT, F, FACE)),
               owners.reshape((-1, FT_DEV, NT, K)),
               margin_weights.reshape((-1, FT_DEV, NT, K)))
    interface = lax.map(tile_group, grouped).reshape((FT, NT, F, FACE))
    face_gradient = time_adjoint(face_rows) + interface
    return cell_gradient, face_gradient
```

```python
import math

import jax
import jax.numpy as jnp
import numpy as np
from jax import lax
from jax.experimental import pallas as pl
from jax.experimental.pallas import tpu as pltpu
from jax.sharding import Mesh
from jax.sharding import PartitionSpec as P

NT = 17
NH = 5
F = 5
FACE = 128
K = 3
TILES = 16
LAYERS = 8
NP = 512
BLOCKS = 512
CAP = 2
ROWS = TILES * NT
WIDTH = F * FACE
SLOTS = BLOCKS * CAP
PEERS = 16
GROUP = BLOCKS // PEERS

SPREAD = ("x", "y")
SHARED = ("z", "core")
RADIAL = ("y", "z", "core")
f32 = jnp.float32
bf16 = jnp.bfloat16


def offset_weights():
    m = np.arange(1, NT // 2 + 1, dtype=np.float64)[:, None]
    h = np.arange(1, NH + 1, dtype=np.float64)[None, :]
    return [float(v) for v in -(2.0 * 0.5 / NT) * np.sum(h * np.sin(2.0 * math.pi * h * m / NT), axis=1)]


def time_sum(values):
    weights = offset_weights()
    out = []
    for t in range(NT):
        total = None
        for m, w in enumerate(weights, start=1):
            term = (values[(t + m) % NT] - values[(t - m) % NT]) * w
            total = term if total is None else total + term
        out.append(total)
    return out


def lane_rows(ref):
    table = ref[...].astype(f32).reshape(K * TILES, NT)
    lane = lax.broadcasted_iota(jnp.int32, (NT, ROWS), 1)
    pick = (lane // TILES == lax.broadcasted_iota(jnp.int32, (NT, ROWS), 0)).astype(f32)
    spread = jnp.dot(table, pick, precision=lax.Precision.HIGHEST, preferred_element_type=f32)
    spread = spread.reshape(K, TILES, ROWS)
    sub = lax.broadcasted_iota(jnp.int32, (K, TILES, ROWS), 1)
    col = lax.broadcasted_iota(jnp.int32, (K, TILES, ROWS), 2)
    return jnp.sum(jnp.where(col % TILES == sub, spread, 0.0), axis=1)


def dispatch_kernel(face_ref, owner_ref, out_ref):
    owner = lane_rows(owner_ref).astype(jnp.int32)
    block = lax.broadcasted_iota(jnp.int32, (BLOCKS, ROWS), 0)
    hit = (owner[0:1] == block) | (owner[1:2] == block) | (owner[2:3] == block)
    hit = jnp.where(hit, 1.0, 0.0)
    earlier = lax.broadcasted_iota(jnp.int32, (ROWS, ROWS), 0) < lax.broadcasted_iota(
        jnp.int32, (ROWS, ROWS), 1
    )
    earlier = jnp.where(earlier, 1.0, 0.0).astype(bf16)
    rank = jnp.dot(hit.astype(bf16), earlier, preferred_element_type=f32)
    first = jnp.where(rank < 0.5, hit, 0.0).reshape(BLOCKS // 8, 8, ROWS)
    second = jnp.where(rank > 0.5, hit, 0.0).reshape(BLOCKS // 8, 8, ROWS)
    select = jnp.stack([first, second], axis=1).reshape(SLOTS, ROWS).astype(bf16)
    rows = [face_ref[:, f].reshape(ROWS, FACE).astype(bf16) for f in range(F)]
    rows = jnp.concatenate(rows, axis=1)
    out_ref[...] = jnp.dot(select, rows, preferred_element_type=f32).astype(bf16)


def weights_kernel(face_ref, owner_ref, margin_ref, high_ref, low_ref, time_ref):
    both = jnp.concatenate([lane_rows(owner_ref), lane_rows(margin_ref), jnp.zeros((2, ROWS), f32)], axis=0)
    both = both.T
    slot = lax.broadcasted_iota(jnp.int32, (ROWS, SLOTS), 1)
    block = (slot // 16 * 8 + slot % 8).astype(f32)
    hit = jnp.zeros((ROWS, SLOTS), f32)
    weight = jnp.zeros((ROWS, SLOTS), f32)
    for k in range(K):
        same = both[:, k : k + 1] == block
        hit = jnp.where(same, 1.0, hit)
        weight = jnp.where(same, both[:, K + k : K + k + 1], weight)
    earlier = lax.broadcasted_iota(jnp.int32, (ROWS, ROWS), 1) < lax.broadcasted_iota(
        jnp.int32, (ROWS, ROWS), 0
    )
    earlier = jnp.where(earlier, 1.0, 0.0).astype(bf16)
    rank = jnp.dot(earlier, hit.astype(bf16), preferred_element_type=f32)
    own = (slot // 8 % 2).astype(f32)
    weight = jnp.where(jnp.abs(rank - own) < 0.5, weight, 0.0)
    high = weight.astype(bf16)
    high_ref[...] = high
    low_ref[...] = (weight - high.astype(f32)).astype(bf16)
    for f in range(F):
        total = time_sum([face_ref[t, f] for t in range(NT)])
        for t in range(NT):
            time_ref[t, f] = total[t]


def maps_kernel(rows_ref, maps_ref, out_ref):
    sub = lax.broadcasted_iota(jnp.int32, (PEERS, 16, FACE), 1) % 8
    for g in range(GROUP // 8):
        maps = maps_ref[8 * g : 8 * g + 8].reshape(8 * FACE, FACE)
        for f in range(F):
            lanes = slice(f * FACE, (f + 1) * FACE)
            rows = rows_ref[:, 16 * g : 16 * g + 16, lanes].astype(f32)
            parts = [jnp.where(sub == q, rows, 0.0).reshape(PEERS * 16, FACE).astype(bf16) for q in range(8)]
            result = jnp.dot(jnp.concatenate(parts, axis=1), maps, preferred_element_type=f32)
            out_ref[:, 16 * g : 16 * g + 16, lanes] = result.astype(bf16).reshape(PEERS, 16, FACE)


def combine_kernel(rows_ref, high_ref, low_ref, time_ref, out_ref):
    rows = rows_ref[...]
    total = jnp.dot(high_ref[...], rows, preferred_element_type=f32)
    total = total + jnp.dot(low_ref[...], rows, preferred_element_type=f32)
    for f in range(F):
        out_ref[:, f] = time_ref[:, f] + total[:, f * FACE : (f + 1) * FACE].reshape(NT, TILES, FACE)


def edges_kernel(cells_ref, dissipation_ref, first_ref, last_ref):
    count = NT * F
    first_ref[...] = cells_ref[pl.ds(0, count, stride=LAYERS), :] * dissipation_ref[0:1, :]
    last_ref[...] = cells_ref[pl.ds(LAYERS - 1, count, stride=LAYERS), :] * dissipation_ref[LAYERS - 1 :, :]


def cells_kernel(cells_ref, jac_ref, dissipation_ref, before_ref, after_ref, out_ref):
    dissipation = dissipation_ref[...]
    layer = lax.broadcasted_iota(jnp.int32, dissipation.shape, 0)
    for g in range(F):
        values = [cells_ref[t, g] for t in range(NT)]
        total = time_sum(values)
        for t in range(NT):
            field = dissipation * values[t]
            at = t * F + g
            lower = jnp.where(layer == 0, before_ref[at : at + 1, :], pltpu.roll(field, 1, 0))
            upper = jnp.where(layer == LAYERS - 1, after_ref[at : at + 1, :], pltpu.roll(field, LAYERS - 1, 0))
            out_ref[t, g] = total[t] - (upper - 2.0 * field + lower)
    for t in range(NT):
        field = [cells_ref[t, f] for f in range(F)]
        for g in range(F):
            total = out_ref[t, g]
            for f in range(F):
                total = total + jac_ref[t, f, g].astype(f32) * field[f]
            out_ref[t, g] = total


def call(kernel, outs, args, flops=0, **more):
    size = sum(math.prod(a.shape) * a.dtype.itemsize for a in (*args, *jax.tree.leaves(outs)))
    return pl.pallas_call(
        kernel,
        out_shape=outs,
        compiler_params=pltpu.CompilerParams(vmem_limit_bytes=24 << 20),
        cost_estimate=pl.CostEstimate(flops=flops, bytes_accessed=size, transcendentals=0),
        **more,
    )(*args)


def body(adjoint_cells, flux_jacobian, dissipation, face_rows, owners, margin_weights, transposed_maps):
    cells = adjoint_cells[0].transpose(1, 2, 0, 3)
    jac = flux_jacobian[0].transpose(1, 2, 3, 0, 4)
    dissipation = dissipation[0]
    faces = face_rows.transpose(1, 2, 0, 3)
    owner = owners.transpose(2, 0, 1)
    margin = margin_weights.transpose(2, 0, 1)
    shape = jax.ShapeDtypeStruct

    maps = lax.all_gather(transposed_maps, SHARED, axis=0, tiled=True)
    outgoing = call(dispatch_kernel, shape((SLOTS, WIDTH), bf16), (faces, owner), 2 * SLOTS * 2 * ROWS * WIDTH)
    arrived = lax.all_to_all(outgoing.reshape(PEERS, SLOTS // PEERS, WIDTH), SPREAD, 0, 0, tiled=True)

    edge = shape((NT * F, NP), f32)
    lanes = 128
    first, last = call(
        edges_kernel,
        (edge, edge),
        (cells.reshape(NT * F * LAYERS, NP), dissipation),
        grid=(NP // lanes,),
        in_specs=[
            pl.BlockSpec((NT * F * LAYERS, lanes), lambda i: (0, i)),
            pl.BlockSpec((LAYERS, lanes), lambda i: (0, i)),
        ],
        out_specs=[pl.BlockSpec((NT * F, lanes), lambda i: (0, i))] * 2,
    )
    size = lax.axis_size(RADIAL)
    before = lax.ppermute(last, RADIAL, [(i, i + 1) for i in range(size - 1)])
    after = lax.ppermute(first, RADIAL, [(i + 1, i) for i in range(size - 1)])

    spread = shape((ROWS, SLOTS), bf16)
    high, low, time_faces = call(
        weights_kernel, (spread, spread, shape(faces.shape, f32)), (faces, owner, margin), 2 * ROWS * ROWS * SLOTS
    )

    products = call(
        maps_kernel, shape((PEERS, SLOTS // PEERS, WIDTH), bf16), (arrived, maps), 2 * SLOTS * F * 8 * FACE * FACE
    )
    returned = lax.all_to_all(products, SPREAD, 0, 0, tiled=True)

    cell_gradient = call(
        cells_kernel,
        shape(cells.shape, f32),
        (cells, jac, dissipation, before, after),
        24 * NT * F * LAYERS * NP,
        grid=(NP // lanes,),
        in_specs=[
            pl.BlockSpec((NT, F, LAYERS, lanes), lambda i: (0, 0, 0, i)),
            pl.BlockSpec((NT, F, F, LAYERS, lanes), lambda i: (0, 0, 0, 0, i)),
            pl.BlockSpec((LAYERS, lanes), lambda i: (0, i)),
            pl.BlockSpec((NT * F, lanes), lambda i: (0, i)),
            pl.BlockSpec((NT * F, lanes), lambda i: (0, i)),
        ],
        out_specs=pl.BlockSpec((NT, F, LAYERS, lanes), lambda i: (0, 0, 0, i)),
    )

    face_gradient = call(
        combine_kernel,
        shape(faces.shape, f32),
        (returned.reshape(SLOTS, WIDTH), high, low, time_faces),
        4 * ROWS * SLOTS * WIDTH,
    )
    return cell_gradient.transpose(2, 0, 1, 3)[None], face_gradient.transpose(2, 0, 1, 3)


def solution(mesh):
    chips = Mesh(mesh.devices.reshape(4, 4, 4, 2), ("x", "y", "z", "core"))
    every = ("x", "y", "z", "core")
    cells, faces = P("x", RADIAL), P(every)
    return jax.shard_map(
        body,
        mesh=chips,
        in_specs=(cells, cells, cells, faces, faces, faces, faces),
        out_specs=(cells, faces),
        check_vma=False,
    )
```

```python
import math

import jax
import jax.numpy as jnp
import numpy as np
from jax import lax
from jax.experimental import pallas as pl
from jax.experimental.pallas import tpu as pltpu
from jax.sharding import Mesh
from jax.sharding import PartitionSpec as P

NT = 17
NH = 5
F = 5
FACE = 128
K = 3
TILES = 16
LAYERS = 8
NP = 512
BLOCKS = 512
CAP = 2
ROWS = TILES * NT
WIDTH = F * FACE
SLOTS = BLOCKS * CAP
PEERS = 16
GROUP = BLOCKS // PEERS

SPREAD = ("x", "y")
STEPS = (0, 1, 3, 2)
PARTS = 4
RADIAL = ("y", "z", "core")
f32 = jnp.float32
bf16 = jnp.bfloat16


def offset_weights():
    m = np.arange(1, NT // 2 + 1, dtype=np.float64)[:, None]
    h = np.arange(1, NH + 1, dtype=np.float64)[None, :]
    return [float(v) for v in -(2.0 * 0.5 / NT) * np.sum(h * np.sin(2.0 * math.pi * h * m / NT), axis=1)]


def time_sum(values):
    weights = offset_weights()
    out = []
    for t in range(NT):
        total = None
        for m, w in enumerate(weights, start=1):
            term = (values[(t + m) % NT] - values[(t - m) % NT]) * w
            total = term if total is None else total + term
        out.append(total)
    return out


def lane_rows(ref):
    table = ref[...].astype(f32).reshape(K * TILES, NT)
    lane = lax.broadcasted_iota(jnp.int32, (NT, ROWS), 1)
    pick = (lane // TILES == lax.broadcasted_iota(jnp.int32, (NT, ROWS), 0)).astype(f32)
    spread = jnp.dot(table, pick, precision=lax.Precision.HIGHEST, preferred_element_type=f32)
    spread = spread.reshape(K, TILES, ROWS)
    sub = lax.broadcasted_iota(jnp.int32, (K, TILES, ROWS), 1)
    col = lax.broadcasted_iota(jnp.int32, (K, TILES, ROWS), 2)
    return jnp.sum(jnp.where(col % TILES == sub, spread, 0.0), axis=1)


def dispatch_kernel(face_hbm, owner_hbm, out_hbm, face_ref, owner_ref, out_ref, face_sem, owner_sem, out_sem):
    owner_copy = pltpu.make_async_copy(owner_hbm, owner_ref, owner_sem)
    face_copy = pltpu.make_async_copy(face_hbm, face_ref, face_sem)
    owner_copy.start()
    face_copy.start()
    earlier = lax.broadcasted_iota(jnp.int32, (ROWS, ROWS), 0) < lax.broadcasted_iota(
        jnp.int32, (ROWS, ROWS), 1
    )
    earlier = jnp.where(earlier, 1.0, 0.0).astype(bf16)
    block = lax.broadcasted_iota(jnp.int32, (BLOCKS, ROWS), 0)
    owner_copy.wait()
    owner = lane_rows(owner_ref).astype(jnp.int32)
    hit = (owner[0:1] == block) | (owner[1:2] == block) | (owner[2:3] == block)
    hit = jnp.where(hit, 1.0, 0.0)
    rank = jnp.dot(hit.astype(bf16), earlier, preferred_element_type=f32)
    first = jnp.where(rank < 0.5, hit, 0.0).reshape(BLOCKS // 8, 8, ROWS)
    second = jnp.where(rank > 0.5, hit, 0.0).reshape(BLOCKS // 8, 8, ROWS)
    select = jnp.stack([first, second], axis=1).reshape(SLOTS, ROWS).astype(bf16)
    face_copy.wait()
    rows = [face_ref[:, f].reshape(ROWS, FACE).astype(bf16) for f in range(F)]
    rows = jnp.concatenate(rows, axis=1)
    copies = []
    for part in range(PARTS):
        piece = slice(part * SLOTS // PARTS, (part + 1) * SLOTS // PARTS)
        out_ref[piece] = jnp.dot(select[piece], rows, preferred_element_type=f32).astype(bf16)
        copies.append(pltpu.make_async_copy(out_ref.at[piece], out_hbm.at[piece], out_sem.at[part]))
        copies[-1].start()
    for copy in copies:
        copy.wait()


def weights_kernel(face_ref, owner_ref, margin_ref, weight_ref, time_ref):
    both = jnp.concatenate([lane_rows(owner_ref), lane_rows(margin_ref), jnp.zeros((2, ROWS), f32)], axis=0)
    both = both.T
    slot = lax.broadcasted_iota(jnp.int32, (ROWS, SLOTS), 1)
    block = (slot // 16 * 8 + slot % 8).astype(f32)
    hit = jnp.zeros((ROWS, SLOTS), f32)
    weight = jnp.zeros((ROWS, SLOTS), f32)
    for k in range(K):
        same = both[:, k : k + 1] == block
        hit = jnp.where(same, 1.0, hit)
        weight = jnp.where(same, both[:, K + k : K + k + 1], weight)
    earlier = lax.broadcasted_iota(jnp.int32, (ROWS, ROWS), 1) < lax.broadcasted_iota(
        jnp.int32, (ROWS, ROWS), 0
    )
    earlier = jnp.where(earlier, 1.0, 0.0).astype(bf16)
    rank = jnp.dot(earlier, hit.astype(bf16), preferred_element_type=f32)
    own = (slot // 8 % 2).astype(f32)
    weight = jnp.where(jnp.abs(rank - own) < 0.5, weight, 0.0)
    high = weight.astype(bf16)
    weight_ref[0] = high
    weight_ref[1] = (weight - high.astype(f32)).astype(bf16)
    for f in range(F):
        total = time_sum([face_ref[t, f] for t in range(NT)])
        for t in range(NT):
            time_ref[t, f] = total[t]


def maps_kernel(rows_ref, *refs):
    pieces, (out_hbm, maps_ref, out_ref, maps_sem, out_sem) = refs[:8], refs[-5:]
    z, core = lax.axis_index("z"), lax.axis_index("core")
    loads = []
    for d in range(4):
        loads.append([pltpu.make_async_copy(pieces[2 * d + i], maps_ref.at[d, i], maps_sem.at[d, i]) for i in range(2)])
        for load in loads[d]:
            load.start()
    sub = lax.broadcasted_iota(jnp.int32, (16, FACE), 0)
    masks = [jnp.where(sub % 4 == q, 1.0, 0.0).astype(bf16) for q in range(4)]
    near = sub % 8 // 4 == core
    stores = []
    for d, step in enumerate(STEPS):
        span = pl.ds(pl.multiple_of((z + (4 - step)) % 4 * 16, 16), 16)
        for load in loads[d]:
            load.wait()
        maps = [maps_ref[d, i].reshape(4 * FACE, FACE) for i in range(2)]
        maps = jnp.concatenate(maps, axis=1)
        for f in range(F):
            lanes = slice(f * FACE, (f + 1) * FACE)
            rows = rows_ref[:, span, lanes]
            parts = [(rows * mask).reshape(PEERS * 16, FACE) for mask in masks]
            result = jnp.dot(jnp.concatenate(parts, axis=1), maps, preferred_element_type=f32)
            result = result.reshape(PEERS, 16, 2 * FACE)
            out_ref[d, :, :, lanes] = jnp.where(near, result[..., :FACE], result[..., FACE:]).astype(bf16)
        stores.append(pltpu.make_async_copy(out_ref.at[d], out_hbm.at[:, span], out_sem.at[d]))
        stores[d].start()
    for store in stores:
        store.wait()


def combine_kernel(rows_ref, weight_hbm, time_hbm, out_hbm, weight_ref, time_ref, out_ref, in_sem, out_sem):
    loads = [pltpu.make_async_copy(weight_hbm.at[i], weight_ref.at[i], in_sem.at[i]) for i in range(2)]
    loads.append(pltpu.make_async_copy(time_hbm, time_ref, in_sem.at[2]))
    for load in loads:
        load.start()
    stores = []
    for i, fields in enumerate(((0, 1), (2, 3), (4,))):
        rows = rows_ref[:, fields[0] * FACE : (fields[-1] + 1) * FACE]
        total = None
        for part in range(2):
            if i == 0:
                loads[part].wait()
            term = jnp.dot(weight_ref[part], rows, preferred_element_type=f32)
            total = term if total is None else total + term
        if i == 0:
            loads[2].wait()
        for j, f in enumerate(fields):
            part = total[:, j * FACE : (j + 1) * FACE].reshape(NT, TILES, FACE)
            out_ref[:, f] = time_ref[:, f] + part
        span = pl.ds(fields[0], len(fields))
        stores.append(pltpu.make_async_copy(out_ref.at[:, span], out_hbm.at[:, span], out_sem.at[i]))
        stores[-1].start()
    for store in stores:
        store.wait()


def edges_kernel(cells_ref, dissipation_ref, first_ref, last_ref):
    count = NT * F
    first_ref[...] = cells_ref[pl.ds(0, count, stride=LAYERS), :] * dissipation_ref[0:1, :]
    last_ref[...] = cells_ref[pl.ds(LAYERS - 1, count, stride=LAYERS), :] * dissipation_ref[LAYERS - 1 :, :]


def cells_kernel(cells_ref, jac_ref, dissipation_ref, before_ref, after_ref, out_ref):
    dissipation = dissipation_ref[...]
    layer = lax.broadcasted_iota(jnp.int32, dissipation.shape, 0)
    for g in range(F):
        values = [cells_ref[t, g] for t in range(NT)]
        total = time_sum(values)
        for t in range(NT):
            field = dissipation * values[t]
            at = t * F + g
            lower = jnp.where(layer == 0, before_ref[at : at + 1, :], pltpu.roll(field, 1, 0))
            upper = jnp.where(layer == LAYERS - 1, after_ref[at : at + 1, :], pltpu.roll(field, LAYERS - 1, 0))
            out_ref[t, g] = total[t] - (upper - 2.0 * field + lower)
    for t in range(NT):
        field = [cells_ref[t, f] for f in range(F)]
        for g in range(F):
            total = out_ref[t, g]
            for f in range(F):
                total = total + jac_ref[t, f, g].astype(f32) * field[f]
            out_ref[t, g] = total


def in_hbm(*values):
    return tuple(pltpu.with_memory_space_constraint(v, pltpu.HBM) for v in values)


def in_vmem(value):
    return pltpu.with_memory_space_constraint(value, pltpu.VMEM)


def call(kernel, outs, args, flops=0, **more):
    size = sum(math.prod(a.shape) * a.dtype.itemsize for a in (*args, *jax.tree.leaves(outs)))
    return pl.pallas_call(
        kernel,
        out_shape=outs,
        compiler_params=pltpu.CompilerParams(vmem_limit_bytes=24 << 20),
        cost_estimate=pl.CostEstimate(flops=flops, bytes_accessed=size, transcendentals=0),
        **more,
    )(*args)


def shift(value, axis, step):
    size = lax.axis_size(axis)
    return lax.ppermute(value, axis, [(i, (i + step) % size) for i in range(size)])


def body(adjoint_cells, flux_jacobian, dissipation, face_rows, owners, margin_weights, transposed_maps):
    cells = adjoint_cells[0].transpose(1, 2, 0, 3)
    jac = flux_jacobian[0].transpose(1, 2, 3, 0, 4)
    dissipation = dissipation[0]
    faces = face_rows.transpose(1, 2, 0, 3)
    owner = owners.transpose(2, 0, 1)
    margin = margin_weights.transpose(2, 0, 1)
    shape = jax.ShapeDtypeStruct
    hbm = pl.BlockSpec(memory_space=pltpu.HBM)
    vmem = pl.BlockSpec(memory_space=pltpu.VMEM)
    dma = pltpu.SemaphoreType.DMA

    outgoing = call(
        dispatch_kernel,
        pltpu.HBM((SLOTS, WIDTH), bf16),
        in_hbm(faces, owner),
        2 * SLOTS * 2 * ROWS * WIDTH,
        in_specs=[hbm, hbm],
        out_specs=hbm,
        scratch_shapes=[
            pltpu.VMEM(faces.shape, f32),
            pltpu.VMEM(owner.shape, jnp.int32),
            pltpu.VMEM((SLOTS, WIDTH), bf16),
            dma,
            dma,
            dma((PARTS,)),
        ],
    )
    arrived = lax.all_to_all(outgoing.reshape(PEERS, SLOTS // PEERS, WIDTH), SPREAD, 0, 0, tiled=True)

    pieces = []
    for step in STEPS:
        piece = shift(transposed_maps, "z", step) if step else transposed_maps
        pieces += [piece, shift(piece, "core", 1)]

    edge = shape((NT * F, NP), f32)
    lanes = 128
    first, last = call(
        edges_kernel,
        (edge, edge),
        in_hbm(cells.reshape(NT * F * LAYERS, NP), dissipation),
        grid=(NP // lanes,),
        in_specs=[
            pl.BlockSpec((NT * F * LAYERS, lanes), lambda i: (0, i)),
            pl.BlockSpec((LAYERS, lanes), lambda i: (0, i)),
        ],
        out_specs=[pl.BlockSpec((NT * F, lanes), lambda i: (0, i))] * 2,
    )
    size = lax.axis_size(RADIAL)
    before = lax.ppermute(last, RADIAL, [(i, i + 1) for i in range(size - 1)])
    after = lax.ppermute(first, RADIAL, [(i + 1, i) for i in range(size - 1)])

    weights, time_faces = call(
        weights_kernel,
        (pltpu.HBM((2, ROWS, SLOTS), bf16), pltpu.HBM(faces.shape, f32)),
        in_hbm(faces, owner, margin),
        2 * ROWS * ROWS * SLOTS,
    )

    before, after = in_hbm(before, after)
    products = call(
        maps_kernel,
        pltpu.HBM((PEERS, SLOTS // PEERS, WIDTH), bf16),
        (in_vmem(arrived), *in_hbm(*pieces), before, after),
        2 * SLOTS * F * 8 * FACE * FACE,
        in_specs=[vmem] + [hbm] * 10,
        out_specs=hbm,
        scratch_shapes=[
            pltpu.VMEM((4, 2, 4, FACE, FACE), bf16),
            pltpu.VMEM((4, PEERS, 16, WIDTH), bf16),
            dma((4, 2)),
            dma((4,)),
        ],
    )
    returned = lax.all_to_all(products, SPREAD, 0, 0, tiled=True)

    cell_gradient = call(
        cells_kernel,
        pltpu.HBM(cells.shape, f32),
        in_hbm(cells, jac, dissipation, before, after),
        24 * NT * F * LAYERS * NP,
        grid=(NP // lanes,),
        in_specs=[
            pl.BlockSpec((NT, F, LAYERS, lanes), lambda i: (0, 0, 0, i)),
            pl.BlockSpec((NT, F, F, LAYERS, lanes), lambda i: (0, 0, 0, 0, i)),
            pl.BlockSpec((LAYERS, lanes), lambda i: (0, i)),
            pl.BlockSpec((NT * F, lanes), lambda i: (0, i)),
            pl.BlockSpec((NT * F, lanes), lambda i: (0, i)),
        ],
        out_specs=pl.BlockSpec((NT, F, LAYERS, lanes), lambda i: (0, 0, 0, i)),
    )

    face_gradient = call(
        combine_kernel,
        pltpu.HBM(faces.shape, f32),
        (in_vmem(returned.reshape(SLOTS, WIDTH)), *in_hbm(weights, time_faces)),
        4 * ROWS * SLOTS * WIDTH,
        in_specs=[vmem, hbm, hbm],
        out_specs=hbm,
        scratch_shapes=[
            pltpu.VMEM((2, ROWS, SLOTS), bf16),
            pltpu.VMEM(faces.shape, f32),
            pltpu.VMEM(faces.shape, f32),
            dma((3,)),
            dma((3,)),
        ],
    )
    return cell_gradient.transpose(2, 0, 1, 3)[None], face_gradient.transpose(2, 0, 1, 3)


def solution(mesh):
    chips = Mesh(mesh.devices.reshape(4, 4, 4, 2), ("x", "y", "z", "core"))
    every = ("x", "y", "z", "core")
    cells, faces = P("x", RADIAL), P(every)
    return jax.shard_map(
        body,
        mesh=chips,
        in_specs=(cells, cells, cells, faces, faces, faces, faces),
        out_specs=(cells, faces),
        check_vma=False,
    )
```

```python
import math

import jax
import jax.numpy as jnp
import numpy as np
from jax import lax
from jax.experimental import pallas as pl
from jax.experimental.pallas import tpu as pltpu
from jax.sharding import Mesh
from jax.sharding import PartitionSpec as P

NT = 17
NH = 5
F = 5
FACE = 128
K = 3
TILES = 16
LAYERS = 8
NP = 512
BLOCKS = 512
CAP = 2
ROWS = TILES * NT
WIDTH = F * FACE
SLOTS = BLOCKS * CAP
PEERS = 16
GROUP = BLOCKS // PEERS

SPREAD = ("x", "y")
STEPS = (0, 1, 3, 2)
PARTS = 4
RADIAL = ("y", "z", "core")
f32 = jnp.float32
bf16 = jnp.bfloat16


def offset_weights():
    m = np.arange(1, NT // 2 + 1, dtype=np.float64)[:, None]
    h = np.arange(1, NH + 1, dtype=np.float64)[None, :]
    return [float(v) for v in -(2.0 * 0.5 / NT) * np.sum(h * np.sin(2.0 * math.pi * h * m / NT), axis=1)]


def time_sum(values):
    weights = offset_weights()
    out = []
    for t in range(NT):
        total = None
        for m, w in enumerate(weights, start=1):
            term = (values[(t + m) % NT] - values[(t - m) % NT]) * w
            total = term if total is None else total + term
        out.append(total)
    return out


def lane_rows(ref):
    table = ref[...].reshape(K * TILES, NT)
    lane = lax.broadcasted_iota(jnp.int32, (NT, ROWS), 1)
    pick = (lane // TILES == lax.broadcasted_iota(jnp.int32, (NT, ROWS), 0)).astype(f32)
    if table.dtype == jnp.int32:
        table = jnp.concatenate([table >> 4, table & 15], axis=0).astype(f32).astype(bf16)
        spread = jnp.dot(table, pick.astype(bf16), preferred_element_type=f32)
        spread = 16.0 * spread[: K * TILES] + spread[K * TILES :]
    else:
        spread = jnp.dot(table, pick, precision=lax.Precision.HIGHEST, preferred_element_type=f32)
    spread = spread.reshape(K, TILES, ROWS)
    sub = lax.broadcasted_iota(jnp.int32, (K, TILES, ROWS), 1)
    col = lax.broadcasted_iota(jnp.int32, (K, TILES, ROWS), 2)
    return jnp.sum(jnp.where(col % TILES == sub, spread, 0.0), axis=1)


def dispatch_kernel(face_hbm, owner_hbm, out_hbm, face_ref, owner_ref, out_ref, face_sem, owner_sem, out_sem):
    owner_copy = pltpu.make_async_copy(owner_hbm, owner_ref, owner_sem)
    face_copy = pltpu.make_async_copy(face_hbm, face_ref, face_sem)
    owner_copy.start()
    face_copy.start()
    earlier = lax.broadcasted_iota(jnp.int32, (ROWS, ROWS), 0) < lax.broadcasted_iota(
        jnp.int32, (ROWS, ROWS), 1
    )
    earlier = jnp.where(earlier, 1.0, 0.0).astype(bf16)
    block = lax.broadcasted_iota(jnp.int32, (BLOCKS, ROWS), 0)
    owner_copy.wait()
    owner = lane_rows(owner_ref).astype(jnp.int32)
    hit = (owner[0:1] == block) | (owner[1:2] == block) | (owner[2:3] == block)
    hit = jnp.where(hit, 1.0, 0.0)
    rank = jnp.dot(hit.astype(bf16), earlier, preferred_element_type=f32)
    first = jnp.where(rank < 0.5, hit, 0.0).reshape(BLOCKS // 8, 8, ROWS)
    second = jnp.where(rank > 0.5, hit, 0.0).reshape(BLOCKS // 8, 8, ROWS)
    select = jnp.stack([first, second], axis=1).reshape(SLOTS, ROWS).astype(bf16)
    face_copy.wait()
    rows = [face_ref[:, f].reshape(ROWS, FACE).astype(bf16) for f in range(F)]
    rows = jnp.concatenate(rows, axis=1)
    copies = []
    for part in range(PARTS):
        piece = slice(part * SLOTS // PARTS, (part + 1) * SLOTS // PARTS)
        out_ref[piece] = jnp.dot(select[piece], rows, preferred_element_type=f32).astype(bf16)
        copies.append(pltpu.make_async_copy(out_ref.at[piece], out_hbm.at[piece], out_sem.at[part]))
        copies[-1].start()
    for copy in copies:
        copy.wait()


def weights_kernel(face_ref, owner_ref, margin_ref, weight_ref, time_ref):
    both = jnp.concatenate([lane_rows(owner_ref), lane_rows(margin_ref), jnp.zeros((2, ROWS), f32)], axis=0)
    both = both.T
    slot = lax.broadcasted_iota(jnp.int32, (ROWS, SLOTS), 1)
    block = (slot // 16 * 8 + slot % 8).astype(f32)
    hit = jnp.zeros((ROWS, SLOTS), f32)
    weight = jnp.zeros((ROWS, SLOTS), f32)
    for k in range(K):
        same = both[:, k : k + 1] == block
        hit = jnp.where(same, 1.0, hit)
        weight = jnp.where(same, both[:, K + k : K + k + 1], weight)
    earlier = lax.broadcasted_iota(jnp.int32, (ROWS, ROWS), 1) < lax.broadcasted_iota(
        jnp.int32, (ROWS, ROWS), 0
    )
    earlier = jnp.where(earlier, 1.0, 0.0).astype(bf16)
    rank = jnp.dot(earlier, hit.astype(bf16), preferred_element_type=f32)
    own = (slot // 8 % 2).astype(f32)
    weight = jnp.where(jnp.abs(rank - own) < 0.5, weight, 0.0)
    high = weight.astype(bf16)
    weight_ref[0] = high
    weight_ref[1] = (weight - high.astype(f32)).astype(bf16)
    for f in range(F):
        total = time_sum([face_ref[t, f] for t in range(NT)])
        for t in range(NT):
            time_ref[t, f] = total[t]


def maps_kernel(rows_ref, *refs):
    pieces, (out_hbm, maps_ref, out_ref, maps_sem, out_sem) = refs[:8], refs[-5:]
    z, core = lax.axis_index("z"), lax.axis_index("core")
    loads = []
    for d in range(4):
        loads.append([pltpu.make_async_copy(pieces[2 * d + i], maps_ref.at[d, i], maps_sem.at[d, i]) for i in range(2)])
        for load in loads[d]:
            load.start()
    sub = lax.broadcasted_iota(jnp.int32, (16, FACE), 0)
    masks = [jnp.where(sub % 4 == q, 1.0, 0.0).astype(bf16) for q in range(4)]
    near = sub % 8 // 4 == core
    stores = []
    for d, step in enumerate(STEPS):
        span = pl.ds(pl.multiple_of((z + (4 - step)) % 4 * 16, 16), 16)
        for load in loads[d]:
            load.wait()
        maps = [maps_ref[d, i].reshape(4 * FACE, FACE) for i in range(2)]
        maps = jnp.concatenate(maps, axis=1)
        for f in range(F):
            lanes = slice(f * FACE, (f + 1) * FACE)
            rows = rows_ref[:, span, lanes]
            parts = [(rows * mask).reshape(PEERS * 16, FACE) for mask in masks]
            result = jnp.dot(jnp.concatenate(parts, axis=1), maps, preferred_element_type=f32)
            result = result.reshape(PEERS, 16, 2 * FACE)
            out_ref[d, :, :, lanes] = jnp.where(near, result[..., :FACE], result[..., FACE:]).astype(bf16)
        stores.append(pltpu.make_async_copy(out_ref.at[d], out_hbm.at[:, span], out_sem.at[d]))
        stores[d].start()
    for store in stores:
        store.wait()


def combine_kernel(rows_ref, weight_hbm, time_hbm, out_hbm, weight_ref, time_ref, out_ref, in_sem, out_sem):
    loads = [pltpu.make_async_copy(weight_hbm.at[i], weight_ref.at[i], in_sem.at[i]) for i in range(2)]
    loads.append(pltpu.make_async_copy(time_hbm, time_ref, in_sem.at[2]))
    for load in loads:
        load.start()
    stores = []
    for i, fields in enumerate(((0, 1), (2, 3), (4,))):
        rows = rows_ref[:, fields[0] * FACE : (fields[-1] + 1) * FACE]
        total = None
        for part in range(2):
            if i == 0:
                loads[part].wait()
            term = jnp.dot(weight_ref[part], rows, preferred_element_type=f32)
            total = term if total is None else total + term
        if i == 0:
            loads[2].wait()
        for j, f in enumerate(fields):
            part = total[:, j * FACE : (j + 1) * FACE].reshape(NT, TILES, FACE)
            out_ref[:, f] = time_ref[:, f] + part
        span = pl.ds(fields[0], len(fields))
        stores.append(pltpu.make_async_copy(out_ref.at[:, span], out_hbm.at[:, span], out_sem.at[i]))
        stores[-1].start()
    for store in stores:
        store.wait()


def edges_kernel(cells_hbm, dissipation_ref, inner_ref, outer_ref, cells_ref, sem):
    lanes = [pl.ds(i * 128, 128) for i in range(NP // 128)]
    loads = [pltpu.make_async_copy(cells_hbm.at[:, l], cells_ref.at[i], sem.at[i]) for i, l in enumerate(lanes)]
    for load in loads:
        load.start()
    core = lax.axis_index("core")
    count = NT * F
    for i, l in enumerate(lanes):
        loads[i].wait()
        first = cells_ref[i, pl.ds(0, count, stride=LAYERS), :] * dissipation_ref[0:1, l]
        last = cells_ref[i, pl.ds(LAYERS - 1, count, stride=LAYERS), :] * dissipation_ref[LAYERS - 1 :, l]
        inner_ref[:, l] = jnp.where(core == 0, last, first)
        outer_ref[:, l] = jnp.where(core == 0, first, last)


def cells_kernel(cells_ref, jac_ref, dissipation_ref, inner_ref, outer_ref, out_ref):
    dissipation = dissipation_ref[...]
    layer = lax.broadcasted_iota(jnp.int32, dissipation.shape, 0)
    core = lax.axis_index("core")
    before = jnp.where(core == 0, outer_ref[...], inner_ref[...])
    after = jnp.where(core == 0, inner_ref[...], outer_ref[...])
    for g in range(F):
        values = [cells_ref[t, g] for t in range(NT)]
        total = time_sum(values)
        for t in range(NT):
            field = dissipation * values[t]
            at = t * F + g
            lower = jnp.where(layer == 0, before[at : at + 1], pltpu.roll(field, 1, 0))
            upper = jnp.where(layer == LAYERS - 1, after[at : at + 1], pltpu.roll(field, LAYERS - 1, 0))
            out_ref[t, g] = total[t] - (upper - 2.0 * field + lower)
    for t in range(NT):
        field = [cells_ref[t, f] for f in range(F)]
        for g in range(F):
            total = out_ref[t, g]
            for f in range(F):
                total = total + jac_ref[t, f, g].astype(f32) * field[f]
            out_ref[t, g] = total


def in_hbm(*values):
    return tuple(pltpu.with_memory_space_constraint(v, pltpu.HBM) for v in values)


def in_vmem(value):
    return pltpu.with_memory_space_constraint(value, pltpu.VMEM)


def call(kernel, outs, args, flops=0, **more):
    size = sum(math.prod(a.shape) * a.dtype.itemsize for a in (*args, *jax.tree.leaves(outs)))
    return pl.pallas_call(
        kernel,
        out_shape=outs,
        compiler_params=pltpu.CompilerParams(vmem_limit_bytes=24 << 20),
        cost_estimate=pl.CostEstimate(flops=flops, bytes_accessed=size, transcendentals=0),
        **more,
    )(*args)


def shift(value, axis, step):
    size = lax.axis_size(axis)
    return lax.ppermute(value, axis, [(i, (i + step) % size) for i in range(size)])


def body(adjoint_cells, flux_jacobian, dissipation, face_rows, owners, margin_weights, transposed_maps):
    cells = adjoint_cells[0].transpose(1, 2, 0, 3)
    jac = flux_jacobian[0].transpose(1, 2, 3, 0, 4)
    dissipation = dissipation[0]
    faces = face_rows.transpose(1, 2, 0, 3)
    owner = owners.transpose(2, 0, 1)
    margin = margin_weights.transpose(2, 0, 1)
    shape = jax.ShapeDtypeStruct
    hbm = pl.BlockSpec(memory_space=pltpu.HBM)
    vmem = pl.BlockSpec(memory_space=pltpu.VMEM)
    dma = pltpu.SemaphoreType.DMA

    outgoing = call(
        dispatch_kernel,
        pltpu.HBM((SLOTS, WIDTH), bf16),
        in_hbm(faces, owner),
        2 * SLOTS * 2 * ROWS * WIDTH,
        in_specs=[hbm, hbm],
        out_specs=hbm,
        scratch_shapes=[
            pltpu.VMEM(faces.shape, f32),
            pltpu.VMEM(owner.shape, jnp.int32),
            pltpu.VMEM((SLOTS, WIDTH), bf16),
            dma,
            dma,
            dma((PARTS,)),
        ],
    )
    arrived = lax.all_to_all(outgoing.reshape(PEERS, SLOTS // PEERS, WIDTH), SPREAD, 0, 0, tiled=True)

    pieces = []
    for step in STEPS:
        piece = shift(transposed_maps, "z", step) if step else transposed_maps
        pieces += [piece, shift(piece, "core", 1)]

    edge = shape((NT * F, NP), f32)
    lanes = 128
    inner, outer = call(
        edges_kernel,
        (edge, edge),
        in_hbm(cells.reshape(NT * F * LAYERS, NP), dissipation),
        in_specs=[hbm, vmem],
        out_specs=[vmem, vmem],
        scratch_shapes=[pltpu.VMEM((NP // lanes, NT * F * LAYERS, lanes), f32), dma((NP // lanes,))],
    )
    joints = [(i, i + 1) for i in range(1, lax.axis_size(RADIAL) - 1, 2)]
    inner = shift(inner, "core", 1)
    outer = lax.ppermute(outer, RADIAL, joints + [(j, i) for i, j in joints])

    weights, time_faces = call(
        weights_kernel,
        (pltpu.HBM((2, ROWS, SLOTS), bf16), pltpu.HBM(faces.shape, f32)),
        in_hbm(faces, owner, margin),
        2 * ROWS * ROWS * SLOTS,
    )

    inner, outer = in_hbm(inner, outer)
    products = call(
        maps_kernel,
        pltpu.HBM((PEERS, SLOTS // PEERS, WIDTH), bf16),
        (in_vmem(arrived), *in_hbm(*pieces), inner, outer),
        2 * SLOTS * F * 8 * FACE * FACE,
        in_specs=[vmem] + [hbm] * 10,
        out_specs=hbm,
        scratch_shapes=[
            pltpu.VMEM((4, 2, 4, FACE, FACE), bf16),
            pltpu.VMEM((4, PEERS, 16, WIDTH), bf16),
            dma((4, 2)),
            dma((4,)),
        ],
    )
    returned = lax.all_to_all(products, SPREAD, 0, 0, tiled=True)

    cell_gradient = call(
        cells_kernel,
        pltpu.HBM(cells.shape, f32),
        in_hbm(cells, jac, dissipation, inner, outer),
        24 * NT * F * LAYERS * NP,
        grid=(NP // lanes,),
        in_specs=[
            pl.BlockSpec((NT, F, LAYERS, lanes), lambda i: (0, 0, 0, i)),
            pl.BlockSpec((NT, F, F, LAYERS, lanes), lambda i: (0, 0, 0, 0, i)),
            pl.BlockSpec((LAYERS, lanes), lambda i: (0, i)),
            pl.BlockSpec((NT * F, lanes), lambda i: (0, i)),
            pl.BlockSpec((NT * F, lanes), lambda i: (0, i)),
        ],
        out_specs=pl.BlockSpec((NT, F, LAYERS, lanes), lambda i: (0, 0, 0, i)),
    )

    face_gradient = call(
        combine_kernel,
        pltpu.HBM(faces.shape, f32),
        (in_vmem(returned.reshape(SLOTS, WIDTH)), *in_hbm(weights, time_faces)),
        4 * ROWS * SLOTS * WIDTH,
        in_specs=[vmem, hbm, hbm],
        out_specs=hbm,
        scratch_shapes=[
            pltpu.VMEM((2, ROWS, SLOTS), bf16),
            pltpu.VMEM(faces.shape, f32),
            pltpu.VMEM(faces.shape, f32),
            dma((3,)),
            dma((3,)),
        ],
    )
    return cell_gradient.transpose(2, 0, 1, 3)[None], face_gradient.transpose(2, 0, 1, 3)


def solution(mesh):
    chips = Mesh(mesh.devices.reshape(4, 4, 4, 2), ("x", "y", "z", "core"))
    every = ("x", "y", "z", "core")
    cells, faces = P("x", RADIAL), P(every)
    return jax.shard_map(
        body,
        mesh=chips,
        in_specs=(cells, cells, cells, faces, faces, faces, faces),
        out_specs=(cells, faces),
        check_vma=False,
    )
```

```python
import math

import jax
import jax.numpy as jnp
import numpy as np
from jax import lax
from jax.experimental import pallas as pl
from jax.experimental.pallas import tpu as pltpu
from jax.sharding import Mesh
from jax.sharding import PartitionSpec as P

NT = 17
NH = 5
F = 5
FACE = 128
K = 3
TILES = 16
LAYERS = 8
NP = 512
BLOCKS = 512
CAP = 2
ROWS = TILES * NT
WIDTH = F * FACE
SLOTS = BLOCKS * CAP
PEERS = 16
GROUP = BLOCKS // PEERS

SPREAD = ("x", "y")
STEPS = (0, 1, 3, 2)
PARTS = 4
RADIAL = ("y", "z", "core")
f32 = jnp.float32
bf16 = jnp.bfloat16


def offset_weights():
    m = np.arange(1, NT // 2 + 1, dtype=np.float64)[:, None]
    h = np.arange(1, NH + 1, dtype=np.float64)[None, :]
    return [float(v) for v in -(2.0 * 0.5 / NT) * np.sum(h * np.sin(2.0 * math.pi * h * m / NT), axis=1)]


def time_sum(values):
    weights = offset_weights()
    out = []
    for t in range(NT):
        total = None
        for m, w in enumerate(weights, start=1):
            term = (values[(t + m) % NT] - values[(t - m) % NT]) * w
            total = term if total is None else total + term
        out.append(total)
    return out


def lane_rows(ref):
    table = ref[...].reshape(K * TILES, NT)
    lane = lax.broadcasted_iota(jnp.int32, (NT, ROWS), 1)
    pick = (lane // TILES == lax.broadcasted_iota(jnp.int32, (NT, ROWS), 0)).astype(f32)
    if table.dtype == jnp.int32:
        table = jnp.concatenate([table >> 4, table & 15], axis=0).astype(f32).astype(bf16)
        spread = jnp.dot(table, pick.astype(bf16), preferred_element_type=f32)
        spread = 16.0 * spread[: K * TILES] + spread[K * TILES :]
    else:
        spread = jnp.dot(table, pick, precision=lax.Precision.HIGHEST, preferred_element_type=f32)
    spread = spread.reshape(K, TILES, ROWS)
    sub = lax.broadcasted_iota(jnp.int32, (K, TILES, ROWS), 1)
    col = lax.broadcasted_iota(jnp.int32, (K, TILES, ROWS), 2)
    return jnp.sum(jnp.where(col % TILES == sub, spread, 0.0), axis=1)


def dispatch_kernel(face_hbm, owner_hbm, out_hbm, face_ref, owner_ref, out_ref, face_sem, owner_sem, out_sem):
    owner_copy = pltpu.make_async_copy(owner_hbm, owner_ref, owner_sem)
    face_copy = pltpu.make_async_copy(face_hbm, face_ref, face_sem)
    owner_copy.start()
    face_copy.start()
    earlier = lax.broadcasted_iota(jnp.int32, (ROWS, ROWS), 0) < lax.broadcasted_iota(
        jnp.int32, (ROWS, ROWS), 1
    )
    earlier = jnp.where(earlier, 1.0, 0.0).astype(bf16)
    block = lax.broadcasted_iota(jnp.int32, (BLOCKS, ROWS), 0)
    owner_copy.wait()
    owner = lane_rows(owner_ref).astype(jnp.int32)
    hit = (owner[0:1] == block) | (owner[1:2] == block) | (owner[2:3] == block)
    hit = jnp.where(hit, 1.0, 0.0)
    rank = jnp.dot(hit.astype(bf16), earlier, preferred_element_type=f32)
    first = jnp.where(rank < 0.5, hit, 0.0).reshape(BLOCKS // 8, 8, ROWS)
    second = jnp.where(rank > 0.5, hit, 0.0).reshape(BLOCKS // 8, 8, ROWS)
    select = jnp.stack([first, second], axis=1).reshape(SLOTS, ROWS).astype(bf16)
    face_copy.wait()
    rows = [face_ref[:, f].reshape(ROWS, FACE).astype(bf16) for f in range(F)]
    rows = jnp.concatenate(rows, axis=1)
    copies = []
    for part in range(PARTS):
        piece = slice(part * SLOTS // PARTS, (part + 1) * SLOTS // PARTS)
        out_ref[piece] = jnp.dot(select[piece], rows, preferred_element_type=f32).astype(bf16)
        copies.append(pltpu.make_async_copy(out_ref.at[piece], out_hbm.at[piece], out_sem.at[part]))
        copies[-1].start()
    for copy in copies:
        copy.wait()


def weights_kernel(face_ref, owner_ref, margin_ref, weight_ref, time_ref):
    both = jnp.concatenate([lane_rows(owner_ref), lane_rows(margin_ref), jnp.zeros((2, ROWS), f32)], axis=0)
    both = both.T
    slot = lax.broadcasted_iota(jnp.int32, (ROWS, SLOTS), 1)
    block = (slot // 16 * 8 + slot % 8).astype(f32)
    hit = jnp.zeros((ROWS, SLOTS), f32)
    weight = jnp.zeros((ROWS, SLOTS), f32)
    for k in range(K):
        same = both[:, k : k + 1] == block
        hit = jnp.where(same, 1.0, hit)
        weight = jnp.where(same, both[:, K + k : K + k + 1], weight)
    earlier = lax.broadcasted_iota(jnp.int32, (ROWS, ROWS), 1) < lax.broadcasted_iota(
        jnp.int32, (ROWS, ROWS), 0
    )
    earlier = jnp.where(earlier, 1.0, 0.0).astype(bf16)
    rank = jnp.dot(earlier, hit.astype(bf16), preferred_element_type=f32)
    own = (slot // 8 % 2).astype(f32)
    weight = jnp.where(jnp.abs(rank - own) < 0.5, weight, 0.0)
    high = weight.astype(bf16)
    weight_ref[0] = high
    weight_ref[1] = (weight - high.astype(f32)).astype(bf16)
    for f in range(F):
        total = time_sum([face_ref[t, f] for t in range(NT)])
        for t in range(NT):
            time_ref[t, f] = total[t]


def maps_kernel(rows_ref, *refs):
    pieces, (out_hbm, maps_ref, out_ref, maps_sem, out_sem) = refs[:8], refs[-5:]
    z, core = lax.axis_index("z"), lax.axis_index("core")
    loads = []
    for d in range(4):
        loads.append([pltpu.make_async_copy(pieces[2 * d + i], maps_ref.at[d, i], maps_sem.at[d, i]) for i in range(2)])
        for load in loads[d]:
            load.start()
    sub = lax.broadcasted_iota(jnp.int32, (16, FACE), 0)
    masks = [jnp.where(sub % 4 == q, 1.0, 0.0).astype(bf16) for q in range(4)]
    near = sub % 8 // 4 == core
    stores = []
    for d, step in enumerate(STEPS):
        span = pl.ds(pl.multiple_of((z + (4 - step)) % 4 * 16, 16), 16)
        for load in loads[d]:
            load.wait()
        maps = [maps_ref[d, i].reshape(4 * FACE, FACE) for i in range(2)]
        maps = jnp.concatenate(maps, axis=1)
        for f in range(F):
            lanes = slice(f * FACE, (f + 1) * FACE)
            rows = rows_ref[:, span, lanes]
            parts = [(rows * mask).reshape(PEERS * 16, FACE) for mask in masks]
            result = jnp.dot(jnp.concatenate(parts, axis=1), maps, preferred_element_type=f32)
            result = result.reshape(PEERS, 16, 2 * FACE)
            out_ref[d, :, :, lanes] = jnp.where(near, result[..., :FACE], result[..., FACE:]).astype(bf16)
        stores.append(pltpu.make_async_copy(out_ref.at[d], out_hbm.at[:, span], out_sem.at[d]))
        stores[d].start()
    for store in stores:
        store.wait()


def combine_kernel(rows_ref, weight_hbm, time_hbm, out_hbm, weight_ref, time_ref, out_ref, in_sem, out_sem):
    loads = [pltpu.make_async_copy(weight_hbm.at[i], weight_ref.at[i], in_sem.at[i]) for i in range(2)]
    loads.append(pltpu.make_async_copy(time_hbm, time_ref, in_sem.at[2]))
    for load in loads:
        load.start()
    stores = []
    for i, fields in enumerate(((0, 1), (2, 3), (4,))):
        rows = rows_ref[:, fields[0] * FACE : (fields[-1] + 1) * FACE]
        total = None
        for part in range(2):
            if i == 0:
                loads[part].wait()
            term = jnp.dot(weight_ref[part], rows, preferred_element_type=f32)
            total = term if total is None else total + term
        if i == 0:
            loads[2].wait()
        for j, f in enumerate(fields):
            part = total[:, j * FACE : (j + 1) * FACE].reshape(NT, TILES, FACE)
            out_ref[:, f] = time_ref[:, f] + part
        span = pl.ds(fields[0], len(fields))
        stores.append(pltpu.make_async_copy(out_ref.at[:, span], out_hbm.at[:, span], out_sem.at[i]))
        stores[-1].start()
    for store in stores:
        store.wait()


def edges_kernel(cells_hbm, dissipation_ref, inner_ref, outer_ref, cells_ref, sem):
    lanes = [pl.ds(i * 128, 128) for i in range(NP // 128)]
    loads = [pltpu.make_async_copy(cells_hbm.at[:, l], cells_ref.at[i], sem.at[i]) for i, l in enumerate(lanes)]
    for load in loads:
        load.start()
    core = lax.axis_index("core")
    count = NT * F
    for i, l in enumerate(lanes):
        loads[i].wait()
        first = cells_ref[i, pl.ds(0, count, stride=LAYERS), :] * dissipation_ref[0:1, l]
        last = cells_ref[i, pl.ds(LAYERS - 1, count, stride=LAYERS), :] * dissipation_ref[LAYERS - 1 :, l]
        inner_ref[:, l] = jnp.where(core == 0, last, first)
        outer_ref[:, l] = jnp.where(core == 0, first, last)


def cells_kernel(cells_ref, jac_ref, dissipation_ref, inner_ref, outer_ref, out_ref):
    dissipation = dissipation_ref[...]
    layer = lax.broadcasted_iota(jnp.int32, dissipation.shape, 0)
    core = lax.axis_index("core")
    place = lax.axis_index("y") * 8 + lax.axis_index("z") * 2 + core
    outer = jnp.where((place == 0) | (place == 31), 0.0, outer_ref[...])
    before = jnp.where(core == 0, outer, inner_ref[...])
    after = jnp.where(core == 0, inner_ref[...], outer)
    for g in range(F):
        values = [cells_ref[t, g] for t in range(NT)]
        total = time_sum(values)
        for t in range(NT):
            field = dissipation * values[t]
            at = t * F + g
            lower = jnp.where(layer == 0, before[at : at + 1], pltpu.roll(field, 1, 0))
            upper = jnp.where(layer == LAYERS - 1, after[at : at + 1], pltpu.roll(field, LAYERS - 1, 0))
            out_ref[t, g] = total[t] - (upper - 2.0 * field + lower)
    for t in range(NT):
        field = [cells_ref[t, f] for f in range(F)]
        for g in range(F):
            total = out_ref[t, g]
            for f in range(F):
                total = total + jac_ref[t, f, g].astype(f32) * field[f]
            out_ref[t, g] = total


def in_hbm(*values):
    return tuple(pltpu.with_memory_space_constraint(v, pltpu.HBM) for v in values)


def in_vmem(value):
    return pltpu.with_memory_space_constraint(value, pltpu.VMEM)


def call(kernel, outs, args, flops=0, **more):
    size = sum(math.prod(a.shape) * a.dtype.itemsize for a in (*args, *jax.tree.leaves(outs)))
    return pl.pallas_call(
        kernel,
        out_shape=outs,
        compiler_params=pltpu.CompilerParams(vmem_limit_bytes=24 << 20),
        cost_estimate=pl.CostEstimate(flops=flops, bytes_accessed=size, transcendentals=0),
        **more,
    )(*args)


def shift(value, axis, step):
    size = lax.axis_size(axis)
    return lax.ppermute(value, axis, [(i, (i + step) % size) for i in range(size)])


def body(adjoint_cells, flux_jacobian, dissipation, face_rows, owners, margin_weights, transposed_maps):
    cells = adjoint_cells[0].transpose(1, 2, 0, 3)
    jac = flux_jacobian[0].transpose(1, 2, 3, 0, 4)
    dissipation = dissipation[0]
    faces = face_rows.transpose(1, 2, 0, 3)
    owner = owners.transpose(2, 0, 1)
    margin = margin_weights.transpose(2, 0, 1)
    shape = jax.ShapeDtypeStruct
    hbm = pl.BlockSpec(memory_space=pltpu.HBM)
    vmem = pl.BlockSpec(memory_space=pltpu.VMEM)
    dma = pltpu.SemaphoreType.DMA

    outgoing = call(
        dispatch_kernel,
        pltpu.HBM((SLOTS, WIDTH), bf16),
        in_hbm(faces, owner),
        2 * SLOTS * 2 * ROWS * WIDTH,
        in_specs=[hbm, hbm],
        out_specs=hbm,
        scratch_shapes=[
            pltpu.VMEM(faces.shape, f32),
            pltpu.VMEM(owner.shape, jnp.int32),
            pltpu.VMEM((SLOTS, WIDTH), bf16),
            dma,
            dma,
            dma((PARTS,)),
        ],
    )
    arrived = lax.all_to_all(outgoing.reshape(PEERS, SLOTS // PEERS, WIDTH), SPREAD, 0, 0, tiled=True)

    pieces = []
    for step in STEPS:
        piece = shift(transposed_maps, "z", step) if step else transposed_maps
        pieces += [piece, shift(piece, "core", 1)]

    edge = shape((NT * F, NP), f32)
    lanes = 128
    inner, outer = call(
        edges_kernel,
        (edge, edge),
        in_hbm(cells.reshape(NT * F * LAYERS, NP), dissipation),
        in_specs=[hbm, vmem],
        out_specs=[vmem, vmem],
        scratch_shapes=[pltpu.VMEM((NP // lanes, NT * F * LAYERS, lanes), f32), dma((NP // lanes,))],
    )
    size = lax.axis_size(RADIAL)
    joints = [(i, (i + 1) % size) for i in range(1, size, 2)]
    inner = shift(inner, "core", 1)
    outer = lax.ppermute(outer, RADIAL, joints + [(j, i) for i, j in joints])

    weights, time_faces = call(
        weights_kernel,
        (pltpu.HBM((2, ROWS, SLOTS), bf16), pltpu.HBM(faces.shape, f32)),
        in_hbm(faces, owner, margin),
        2 * ROWS * ROWS * SLOTS,
    )

    inner, outer = in_hbm(inner, outer)
    products = call(
        maps_kernel,
        pltpu.HBM((PEERS, SLOTS // PEERS, WIDTH), bf16),
        (in_vmem(arrived), *in_hbm(*pieces), inner, outer),
        2 * SLOTS * F * 8 * FACE * FACE,
        in_specs=[vmem] + [hbm] * 10,
        out_specs=hbm,
        scratch_shapes=[
            pltpu.VMEM((4, 2, 4, FACE, FACE), bf16),
            pltpu.VMEM((4, PEERS, 16, WIDTH), bf16),
            dma((4, 2)),
            dma((4,)),
        ],
    )
    returned = lax.all_to_all(products, SPREAD, 0, 0, tiled=True)

    cell_gradient = call(
        cells_kernel,
        pltpu.HBM(cells.shape, f32),
        in_hbm(cells, jac, dissipation, inner, outer),
        24 * NT * F * LAYERS * NP,
        grid=(NP // lanes,),
        in_specs=[
            pl.BlockSpec((NT, F, LAYERS, lanes), lambda i: (0, 0, 0, i)),
            pl.BlockSpec((NT, F, F, LAYERS, lanes), lambda i: (0, 0, 0, 0, i)),
            pl.BlockSpec((LAYERS, lanes), lambda i: (0, i)),
            pl.BlockSpec((NT * F, lanes), lambda i: (0, i)),
            pl.BlockSpec((NT * F, lanes), lambda i: (0, i)),
        ],
        out_specs=pl.BlockSpec((NT, F, LAYERS, lanes), lambda i: (0, 0, 0, i)),
    )

    face_gradient = call(
        combine_kernel,
        pltpu.HBM(faces.shape, f32),
        (in_vmem(returned.reshape(SLOTS, WIDTH)), *in_hbm(weights, time_faces)),
        4 * ROWS * SLOTS * WIDTH,
        in_specs=[vmem, hbm, hbm],
        out_specs=hbm,
        scratch_shapes=[
            pltpu.VMEM((2, ROWS, SLOTS), bf16),
            pltpu.VMEM(faces.shape, f32),
            pltpu.VMEM(faces.shape, f32),
            dma((3,)),
            dma((3,)),
        ],
    )
    return cell_gradient.transpose(2, 0, 1, 3)[None], face_gradient.transpose(2, 0, 1, 3)


def solution(mesh):
    chips = Mesh(mesh.devices.reshape(4, 4, 4, 2), ("x", "y", "z", "core"))
    every = ("x", "y", "z", "core")
    cells, faces = P("x", RADIAL), P(every)
    return jax.shard_map(
        body,
        mesh=chips,
        in_specs=(cells, cells, cells, faces, faces, faces, faces),
        out_specs=(cells, faces),
        check_vma=False,
    )
```

```python
import math

import jax
import jax.numpy as jnp
import numpy as np
from jax import lax
from jax.experimental import pallas as pl
from jax.experimental.pallas import tpu as pltpu
from jax.sharding import Mesh
from jax.sharding import PartitionSpec as P

NT = 17
NH = 5
F = 5
FACE = 128
K = 3
TILES = 16
LAYERS = 8
NP = 512
BLOCKS = 512
CAP = 2
ROWS = TILES * NT
WIDTH = F * FACE
SLOTS = BLOCKS * CAP
PEERS = 16
GROUP = BLOCKS // PEERS

SPREAD = ("x", "y")
STEPS = (0, 1, 3, 2)
PARTS = 4
RADIAL = ("y", "z", "core")
f32 = jnp.float32
bf16 = jnp.bfloat16


def offset_weights():
    m = np.arange(1, NT // 2 + 1, dtype=np.float64)[:, None]
    h = np.arange(1, NH + 1, dtype=np.float64)[None, :]
    return [float(v) for v in -(2.0 * 0.5 / NT) * np.sum(h * np.sin(2.0 * math.pi * h * m / NT), axis=1)]


def time_sum(values):
    weights = offset_weights()
    out = []
    for t in range(NT):
        total = None
        for m, w in enumerate(weights, start=1):
            term = (values[(t + m) % NT] - values[(t - m) % NT]) * w
            total = term if total is None else total + term
        out.append(total)
    return out


def lane_rows(ref):
    table = ref[...].reshape(K * TILES, NT)
    lane = lax.broadcasted_iota(jnp.int32, (NT, ROWS), 1)
    pick = (lane // TILES == lax.broadcasted_iota(jnp.int32, (NT, ROWS), 0)).astype(f32)
    if table.dtype == jnp.int32:
        table = jnp.concatenate([table >> 4, table & 15], axis=0).astype(f32).astype(bf16)
        spread = jnp.dot(table, pick.astype(bf16), preferred_element_type=f32)
        spread = 16.0 * spread[: K * TILES] + spread[K * TILES :]
    else:
        spread = jnp.dot(table, pick, precision=lax.Precision.HIGHEST, preferred_element_type=f32)
    spread = spread.reshape(K, TILES, ROWS)
    sub = lax.broadcasted_iota(jnp.int32, (K, TILES, ROWS), 1)
    col = lax.broadcasted_iota(jnp.int32, (K, TILES, ROWS), 2)
    return jnp.sum(jnp.where(col % TILES == sub, spread, 0.0), axis=1)


def dispatch_kernel(face_hbm, owner_hbm, out_hbm, face_ref, owner_ref, out_ref, face_sem, owner_sem, out_sem):
    owner_copy = pltpu.make_async_copy(owner_hbm, owner_ref, owner_sem)
    face_copy = pltpu.make_async_copy(face_hbm, face_ref, face_sem)
    owner_copy.start()
    face_copy.start()
    earlier = lax.broadcasted_iota(jnp.int32, (ROWS, ROWS), 0) < lax.broadcasted_iota(
        jnp.int32, (ROWS, ROWS), 1
    )
    earlier = jnp.where(earlier, 1.0, 0.0).astype(bf16)
    block = lax.broadcasted_iota(jnp.int32, (BLOCKS, ROWS), 0)
    owner_copy.wait()
    owner = lane_rows(owner_ref).astype(jnp.int32)
    hit = (owner[0:1] == block) | (owner[1:2] == block) | (owner[2:3] == block)
    hit = jnp.where(hit, 1.0, 0.0)
    rank = jnp.dot(hit.astype(bf16), earlier, preferred_element_type=f32)
    first = jnp.where(rank < 0.5, hit, 0.0).reshape(BLOCKS // 8, 8, ROWS)
    second = jnp.where(rank > 0.5, hit, 0.0).reshape(BLOCKS // 8, 8, ROWS)
    select = jnp.stack([first, second], axis=1).reshape(SLOTS, ROWS).astype(bf16)
    face_copy.wait()
    rows = [face_ref[:, f].reshape(ROWS, FACE).astype(bf16) for f in range(F)]
    rows = jnp.concatenate(rows, axis=1)
    copies = []
    for part in range(PARTS):
        piece = slice(part * SLOTS // PARTS, (part + 1) * SLOTS // PARTS)
        out_ref[piece] = jnp.dot(select[piece], rows, preferred_element_type=f32).astype(bf16)
        copies.append(pltpu.make_async_copy(out_ref.at[piece], out_hbm.at[piece], out_sem.at[part]))
        copies[-1].start()
    for copy in copies:
        copy.wait()


def weights_kernel(face_ref, owner_ref, margin_ref, weight_ref, time_ref):
    both = jnp.concatenate([lane_rows(owner_ref), lane_rows(margin_ref), jnp.zeros((2, ROWS), f32)], axis=0)
    both = both.T
    slot = lax.broadcasted_iota(jnp.int32, (ROWS, SLOTS), 1)
    block = (slot // 16 * 8 + slot % 8).astype(f32)
    hit = jnp.zeros((ROWS, SLOTS), f32)
    weight = jnp.zeros((ROWS, SLOTS), f32)
    for k in range(K):
        same = both[:, k : k + 1] == block
        hit = jnp.where(same, 1.0, hit)
        weight = jnp.where(same, both[:, K + k : K + k + 1], weight)
    earlier = lax.broadcasted_iota(jnp.int32, (ROWS, ROWS), 1) < lax.broadcasted_iota(
        jnp.int32, (ROWS, ROWS), 0
    )
    earlier = jnp.where(earlier, 1.0, 0.0).astype(bf16)
    rank = jnp.dot(earlier, hit.astype(bf16), preferred_element_type=f32)
    own = (slot // 8 % 2).astype(f32)
    weight = jnp.where(jnp.abs(rank - own) < 0.5, weight, 0.0)
    high = weight.astype(bf16)
    weight_ref[0] = high
    weight_ref[1] = (weight - high.astype(f32)).astype(bf16)
    for f in range(F):
        total = time_sum([face_ref[t, f] for t in range(NT)])
        for t in range(NT):
            time_ref[t, f] = total[t]


def maps_kernel(rows_ref, *refs):
    pieces, (out_hbm, maps_ref, out_ref, maps_sem, out_sem) = refs[:8], refs[-5:]
    z, core = lax.axis_index("z"), lax.axis_index("core")
    loads = []
    for d in range(4):
        loads.append([pltpu.make_async_copy(pieces[2 * d + i], maps_ref.at[d, i], maps_sem.at[d, i]) for i in range(2)])
        for load in loads[d]:
            load.start()
    sub = lax.broadcasted_iota(jnp.int32, (16, FACE), 0)
    masks = [jnp.where(sub % 4 == q, 1.0, 0.0).astype(bf16) for q in range(4)]
    near = sub % 8 // 4 == core
    stores = []
    for d, step in enumerate(STEPS):
        span = pl.ds(pl.multiple_of((z + (4 - step)) % 4 * 16, 16), 16)
        for load in loads[d]:
            load.wait()
        maps = [maps_ref[d, i].reshape(4 * FACE, FACE) for i in range(2)]
        maps = jnp.concatenate(maps, axis=1)
        for f in range(F):
            lanes = slice(f * FACE, (f + 1) * FACE)
            rows = rows_ref[:, span, lanes]
            parts = [(rows * mask).reshape(PEERS * 16, FACE) for mask in masks]
            result = jnp.dot(jnp.concatenate(parts, axis=1), maps, preferred_element_type=f32)
            result = result.reshape(PEERS, 16, 2 * FACE)
            out_ref[d, :, :, lanes] = jnp.where(near, result[..., :FACE], result[..., FACE:]).astype(bf16)
        stores.append(pltpu.make_async_copy(out_ref.at[d], out_hbm.at[:, span], out_sem.at[d]))
        stores[d].start()
    for store in stores:
        store.wait()


def combine_kernel(rows_ref, weight_hbm, time_hbm, out_hbm, weight_ref, time_ref, out_ref, in_sem, out_sem):
    loads = [pltpu.make_async_copy(weight_hbm.at[i], weight_ref.at[i], in_sem.at[i]) for i in range(2)]
    loads.append(pltpu.make_async_copy(time_hbm, time_ref, in_sem.at[2]))
    for load in loads:
        load.start()
    stores = []
    for i, fields in enumerate(((0, 1), (2, 3), (4,))):
        rows = rows_ref[:, fields[0] * FACE : (fields[-1] + 1) * FACE]
        total = None
        for part in range(2):
            if i == 0:
                loads[part].wait()
            term = jnp.dot(weight_ref[part], rows, preferred_element_type=f32)
            total = term if total is None else total + term
        if i == 0:
            loads[2].wait()
        for j, f in enumerate(fields):
            part = total[:, j * FACE : (j + 1) * FACE].reshape(NT, TILES, FACE)
            out_ref[:, f] = time_ref[:, f] + part
        span = pl.ds(fields[0], len(fields))
        stores.append(pltpu.make_async_copy(out_ref.at[:, span], out_hbm.at[:, span], out_sem.at[i]))
        stores[-1].start()
    for store in stores:
        store.wait()


def edges_kernel(cells_hbm, dissipation_ref, inner_ref, outer_ref, cells_ref, sem):
    lanes = [pl.ds(i * 128, 128) for i in range(NP // 128)]
    loads = [pltpu.make_async_copy(cells_hbm.at[:, l], cells_ref.at[i], sem.at[i]) for i, l in enumerate(lanes)]
    for load in loads:
        load.start()
    core = lax.axis_index("core")
    count = NT * F
    for i, l in enumerate(lanes):
        loads[i].wait()
        first = cells_ref[i, pl.ds(0, count, stride=LAYERS), :] * dissipation_ref[0:1, l]
        last = cells_ref[i, pl.ds(LAYERS - 1, count, stride=LAYERS), :] * dissipation_ref[LAYERS - 1 :, l]
        inner_ref[:, l] = jnp.where(core == 0, last, first)
        outer_ref[:, l] = jnp.where(core == 0, first, last)


def cells_kernel(cells_ref, jac_ref, dissipation_ref, inner_ref, outer_ref, out_ref):
    dissipation = dissipation_ref[...]
    layer = lax.broadcasted_iota(jnp.int32, dissipation.shape, 0)
    core = lax.axis_index("core")
    place = lax.axis_index("y") * 8 + lax.axis_index("z") * 2 + core
    outer = jnp.where((place == 0) | (place == 31), 0.0, outer_ref[...])
    before = jnp.where(core == 0, outer, inner_ref[...])
    after = jnp.where(core == 0, inner_ref[...], outer)
    for g in range(F):
        values = [cells_ref[t, g] for t in range(NT)]
        total = time_sum(values)
        for t in range(NT):
            field = dissipation * values[t]
            at = t * F + g
            lower = jnp.where(layer == 0, before[at : at + 1], pltpu.roll(field, 1, 0))
            upper = jnp.where(layer == LAYERS - 1, after[at : at + 1], pltpu.roll(field, LAYERS - 1, 0))
            out_ref[t, g] = total[t] - (upper - 2.0 * field + lower)
    for t in range(NT):
        field = [cells_ref[t, f] for f in range(F)]
        for g in range(F):
            total = out_ref[t, g]
            for f in range(F):
                total = total + jac_ref[t, f, g].astype(f32) * field[f]
            out_ref[t, g] = total


def in_hbm(*values):
    return tuple(pltpu.with_memory_space_constraint(v, pltpu.HBM) for v in values)


def in_vmem(value):
    return pltpu.with_memory_space_constraint(value, pltpu.VMEM)


def call(kernel, outs, args, flops=0, **more):
    size = sum(math.prod(a.shape) * a.dtype.itemsize for a in (*args, *jax.tree.leaves(outs)))
    return pl.pallas_call(
        kernel,
        out_shape=outs,
        compiler_params=pltpu.CompilerParams(vmem_limit_bytes=24 << 20),
        cost_estimate=pl.CostEstimate(flops=flops, bytes_accessed=size, transcendentals=0),
        **more,
    )(*args)


def shift(value, axis, step):
    size = lax.axis_size(axis)
    return lax.ppermute(value, axis, [(i, (i + step) % size) for i in range(size)])


def body(adjoint_cells, flux_jacobian, dissipation, face_rows, owners, margin_weights, transposed_maps):
    cells = adjoint_cells[0].transpose(1, 2, 0, 3)
    jac = flux_jacobian[0].transpose(1, 2, 3, 0, 4)
    dissipation = dissipation[0]
    faces = face_rows.transpose(1, 2, 0, 3)
    owner = owners.transpose(2, 0, 1)
    margin = margin_weights.transpose(2, 0, 1)
    shape = jax.ShapeDtypeStruct
    hbm = pl.BlockSpec(memory_space=pltpu.HBM)
    vmem = pl.BlockSpec(memory_space=pltpu.VMEM)
    dma = pltpu.SemaphoreType.DMA

    outgoing = call(
        dispatch_kernel,
        pltpu.HBM((SLOTS, WIDTH), bf16),
        in_hbm(faces, owner),
        2 * SLOTS * 2 * ROWS * WIDTH,
        in_specs=[hbm, hbm],
        out_specs=hbm,
        scratch_shapes=[
            pltpu.VMEM(faces.shape, f32),
            pltpu.VMEM(owner.shape, jnp.int32),
            pltpu.VMEM((SLOTS, WIDTH), bf16),
            dma,
            dma,
            dma((PARTS,)),
        ],
    )
    arrived = lax.all_to_all(outgoing.reshape(PEERS, SLOTS // PEERS, WIDTH), SPREAD, 0, 0, tiled=True)

    pieces = []
    for step in STEPS:
        piece = shift(transposed_maps, "z", step) if step else transposed_maps
        pieces += [piece, shift(piece, "core", 1)]

    edge = shape((NT * F, NP), f32)
    lanes = 128
    inner, outer = call(
        edges_kernel,
        (edge, edge),
        in_hbm(cells.reshape(NT * F * LAYERS, NP), dissipation),
        in_specs=[hbm, vmem],
        out_specs=[vmem, vmem],
        scratch_shapes=[pltpu.VMEM((NP // lanes, NT * F * LAYERS, lanes), f32), dma((NP // lanes,))],
    )
    size = lax.axis_size(RADIAL)
    inner, relayed = shift(inner, "core", 1), shift(outer, "core", 1)
    outer = lax.ppermute(relayed, RADIAL, [(i, (i + 2 - 4 * (i % 2)) % size) for i in range(size)])

    weights, time_faces = call(
        weights_kernel,
        (pltpu.HBM((2, ROWS, SLOTS), bf16), pltpu.HBM(faces.shape, f32)),
        in_hbm(faces, owner, margin),
        2 * ROWS * ROWS * SLOTS,
    )

    (outer,) = in_hbm(outer)
    products = call(
        maps_kernel,
        pltpu.HBM((PEERS, SLOTS // PEERS, WIDTH), bf16),
        (in_vmem(arrived), *in_hbm(*pieces), outer),
        2 * SLOTS * F * 8 * FACE * FACE,
        in_specs=[vmem] + [hbm] * 9,
        out_specs=hbm,
        scratch_shapes=[
            pltpu.VMEM((4, 2, 4, FACE, FACE), bf16),
            pltpu.VMEM((4, PEERS, 16, WIDTH), bf16),
            dma((4, 2)),
            dma((4,)),
        ],
    )
    returned = lax.all_to_all(products, SPREAD, 0, 0, tiled=True)

    cell_gradient = call(
        cells_kernel,
        pltpu.HBM(cells.shape, f32),
        in_hbm(cells, jac, dissipation, inner, outer),
        24 * NT * F * LAYERS * NP,
        grid=(NP // lanes,),
        in_specs=[
            pl.BlockSpec((NT, F, LAYERS, lanes), lambda i: (0, 0, 0, i)),
            pl.BlockSpec((NT, F, F, LAYERS, lanes), lambda i: (0, 0, 0, 0, i)),
            pl.BlockSpec((LAYERS, lanes), lambda i: (0, i)),
            pl.BlockSpec((NT * F, lanes), lambda i: (0, i)),
            pl.BlockSpec((NT * F, lanes), lambda i: (0, i)),
        ],
        out_specs=pl.BlockSpec((NT, F, LAYERS, lanes), lambda i: (0, 0, 0, i)),
    )

    face_gradient = call(
        combine_kernel,
        pltpu.HBM(faces.shape, f32),
        (in_vmem(returned.reshape(SLOTS, WIDTH)), *in_hbm(weights, time_faces)),
        4 * ROWS * SLOTS * WIDTH,
        in_specs=[vmem, hbm, hbm],
        out_specs=hbm,
        scratch_shapes=[
            pltpu.VMEM((2, ROWS, SLOTS), bf16),
            pltpu.VMEM(faces.shape, f32),
            pltpu.VMEM(faces.shape, f32),
            dma((3,)),
            dma((3,)),
        ],
    )
    return cell_gradient.transpose(2, 0, 1, 3)[None], face_gradient.transpose(2, 0, 1, 3)


def solution(mesh):
    chips = Mesh(mesh.devices.reshape(4, 4, 4, 2), ("x", "y", "z", "core"))
    every = ("x", "y", "z", "core")
    cells, faces = P("x", RADIAL), P(every)
    return jax.shard_map(
        body,
        mesh=chips,
        in_specs=(cells, cells, cells, faces, faces, faces, faces),
        out_specs=(cells, faces),
        check_vma=False,
    )
```

```python
import math

import jax
import jax.numpy as jnp
import numpy as np
from jax import lax
from jax.experimental import pallas as pl
from jax.experimental.pallas import tpu as pltpu
from jax.sharding import Mesh
from jax.sharding import PartitionSpec as P

NT = 17
NH = 5
F = 5
FACE = 128
K = 3
TILES = 16
LAYERS = 8
NP = 512
BLOCKS = 512
CAP = 2
ROWS = TILES * NT
WIDTH = F * FACE
SLOTS = BLOCKS * CAP
PEERS = 16
GROUP = BLOCKS // PEERS

SPREAD = ("x", "y")
STEPS = (0, 1, 3, 2)
PARTS = 2
RADIAL = ("y", "z", "core")
f32 = jnp.float32
bf16 = jnp.bfloat16


def offset_weights():
    m = np.arange(1, NT // 2 + 1, dtype=np.float64)[:, None]
    h = np.arange(1, NH + 1, dtype=np.float64)[None, :]
    return [float(v) for v in -(2.0 * 0.5 / NT) * np.sum(h * np.sin(2.0 * math.pi * h * m / NT), axis=1)]


def time_sum(values):
    weights = offset_weights()
    out = []
    for t in range(NT):
        total = None
        for m, w in enumerate(weights, start=1):
            term = (values[(t + m) % NT] - values[(t - m) % NT]) * w
            total = term if total is None else total + term
        out.append(total)
    return out


def lane_rows(ref):
    table = ref[...].reshape(K * TILES, NT)
    lane = lax.broadcasted_iota(jnp.int32, (NT, ROWS), 1)
    pick = (lane // TILES == lax.broadcasted_iota(jnp.int32, (NT, ROWS), 0)).astype(f32)
    if table.dtype == jnp.int32:
        table = jnp.concatenate([table >> 4, table & 15], axis=0).astype(f32).astype(bf16)
        spread = jnp.dot(table, pick.astype(bf16), preferred_element_type=f32)
        spread = 16.0 * spread[: K * TILES] + spread[K * TILES :]
    else:
        spread = jnp.dot(table, pick, precision=lax.Precision.HIGHEST, preferred_element_type=f32)
    spread = spread.reshape(K, TILES, ROWS)
    sub = lax.broadcasted_iota(jnp.int32, (K, TILES, ROWS), 1)
    col = lax.broadcasted_iota(jnp.int32, (K, TILES, ROWS), 2)
    return jnp.sum(jnp.where(col % TILES == sub, spread, 0.0), axis=1)


def dispatch_kernel(face_hbm, owner_hbm, out_hbm, face_ref, owner_ref, out_ref, face_sem, owner_sem, out_sem):
    owner_copy = pltpu.make_async_copy(owner_hbm, owner_ref, owner_sem)
    face_copy = pltpu.make_async_copy(face_hbm, face_ref, face_sem)
    owner_copy.start()
    face_copy.start()
    earlier = lax.broadcasted_iota(jnp.int32, (ROWS, ROWS), 0) < lax.broadcasted_iota(
        jnp.int32, (ROWS, ROWS), 1
    )
    earlier = jnp.where(earlier, 1.0, 0.0).astype(bf16)
    block = lax.broadcasted_iota(jnp.int32, (BLOCKS, ROWS), 0)
    owner_copy.wait()
    owner = lane_rows(owner_ref).astype(jnp.int32)
    hit = (owner[0:1] == block) | (owner[1:2] == block) | (owner[2:3] == block)
    hit = jnp.where(hit, 1.0, 0.0)
    rank = jnp.dot(hit.astype(bf16), earlier, preferred_element_type=f32)
    first = jnp.where(rank < 0.5, hit, 0.0).reshape(BLOCKS // 8, 8, ROWS)
    second = jnp.where(rank > 0.5, hit, 0.0).reshape(BLOCKS // 8, 8, ROWS)
    select = jnp.stack([first, second], axis=1).reshape(SLOTS, ROWS).astype(bf16)
    face_copy.wait()
    rows = [face_ref[:, f].reshape(ROWS, FACE).astype(bf16) for f in range(F)]
    rows = jnp.concatenate(rows, axis=1)
    copies = []
    for part in range(PARTS):
        piece = slice(part * SLOTS // PARTS, (part + 1) * SLOTS // PARTS)
        out_ref[piece] = jnp.dot(select[piece], rows, preferred_element_type=f32).astype(bf16)
        copies.append(pltpu.make_async_copy(out_ref.at[piece], out_hbm.at[piece], out_sem.at[part]))
        copies[-1].start()
    for copy in copies:
        copy.wait()


def weights_kernel(face_ref, owner_ref, margin_ref, weight_ref, time_ref):
    both = jnp.concatenate([lane_rows(owner_ref), lane_rows(margin_ref), jnp.zeros((2, ROWS), f32)], axis=0)
    both = both.T
    slot = lax.broadcasted_iota(jnp.int32, (ROWS, SLOTS), 1)
    block = (slot // 16 * 8 + slot % 8).astype(f32)
    hit = jnp.zeros((ROWS, SLOTS), f32)
    weight = jnp.zeros((ROWS, SLOTS), f32)
    for k in range(K):
        same = both[:, k : k + 1] == block
        hit = jnp.where(same, 1.0, hit)
        weight = jnp.where(same, both[:, K + k : K + k + 1], weight)
    earlier = lax.broadcasted_iota(jnp.int32, (ROWS, ROWS), 1) < lax.broadcasted_iota(
        jnp.int32, (ROWS, ROWS), 0
    )
    earlier = jnp.where(earlier, 1.0, 0.0).astype(bf16)
    rank = jnp.dot(earlier, hit.astype(bf16), preferred_element_type=f32)
    own = (slot // 8 % 2).astype(f32)
    weight = jnp.where(jnp.abs(rank - own) < 0.5, weight, 0.0)
    high = weight.astype(bf16)
    weight_ref[0] = high
    weight_ref[1] = (weight - high.astype(f32)).astype(bf16)
    for f in range(F):
        total = time_sum([face_ref[t, f] for t in range(NT)])
        for t in range(NT):
            time_ref[t, f] = total[t]


def maps_kernel(rows_ref, *refs):
    pieces, (out_hbm, maps_ref, out_ref, maps_sem, out_sem) = refs[:8], refs[-5:]
    z, core = lax.axis_index("z"), lax.axis_index("core")
    loads = []
    for d in range(4):
        loads.append([pltpu.make_async_copy(pieces[2 * d + i], maps_ref.at[d, i], maps_sem.at[d, i]) for i in range(2)])
        for load in loads[d]:
            load.start()
    sub = lax.broadcasted_iota(jnp.int32, (16, FACE), 0)
    masks = [jnp.where(sub % 4 == q, 1.0, 0.0).astype(bf16) for q in range(4)]
    near = sub % 8 // 4 == core
    stores = []
    for d, step in enumerate(STEPS):
        span = pl.ds(pl.multiple_of((z + (4 - step)) % 4 * 16, 16), 16)
        for load in loads[d]:
            load.wait()
        maps = [maps_ref[d, i].reshape(4 * FACE, FACE) for i in range(2)]
        maps = jnp.concatenate(maps, axis=1)
        for f in range(F):
            lanes = slice(f * FACE, (f + 1) * FACE)
            rows = rows_ref[:, span, lanes]
            parts = [(rows * mask).reshape(PEERS * 16, FACE) for mask in masks]
            result = jnp.dot(jnp.concatenate(parts, axis=1), maps, preferred_element_type=f32)
            result = result.reshape(PEERS, 16, 2 * FACE)
            out_ref[d, :, :, lanes] = jnp.where(near, result[..., :FACE], result[..., FACE:]).astype(bf16)
        stores.append(pltpu.make_async_copy(out_ref.at[d], out_hbm.at[:, span], out_sem.at[d]))
        stores[d].start()
    for store in stores:
        store.wait()


def combine_kernel(rows_ref, weight_hbm, time_hbm, out_hbm, weight_ref, time_ref, out_ref, in_sem, out_sem):
    loads = [pltpu.make_async_copy(weight_hbm.at[i], weight_ref.at[i], in_sem.at[i]) for i in range(2)]
    loads.append(pltpu.make_async_copy(time_hbm, time_ref, in_sem.at[2]))
    for load in loads:
        load.start()
    stores = []
    for i, fields in enumerate(((0, 1), (2, 3), (4,))):
        rows = rows_ref[:, fields[0] * FACE : (fields[-1] + 1) * FACE]
        total = None
        for part in range(2):
            if i == 0:
                loads[part].wait()
            term = jnp.dot(weight_ref[part], rows, preferred_element_type=f32)
            total = term if total is None else total + term
        if i == 0:
            loads[2].wait()
        for j, f in enumerate(fields):
            part = total[:, j * FACE : (j + 1) * FACE].reshape(NT, TILES, FACE)
            out_ref[:, f] = time_ref[:, f] + part
        span = pl.ds(fields[0], len(fields))
        stores.append(pltpu.make_async_copy(out_ref.at[:, span], out_hbm.at[:, span], out_sem.at[i]))
        stores[-1].start()
    for store in stores:
        store.wait()


def edges_kernel(cells_hbm, dissipation_ref, inner_ref, outer_ref, cells_ref, sem):
    lanes = [pl.ds(i * 128, 128) for i in range(NP // 128)]
    loads = [pltpu.make_async_copy(cells_hbm.at[:, l], cells_ref.at[i], sem.at[i]) for i, l in enumerate(lanes)]
    for load in loads:
        load.start()
    core = lax.axis_index("core")
    count = NT * F
    for i, l in enumerate(lanes):
        loads[i].wait()
        first = cells_ref[i, pl.ds(0, count, stride=LAYERS), :] * dissipation_ref[0:1, l]
        last = cells_ref[i, pl.ds(LAYERS - 1, count, stride=LAYERS), :] * dissipation_ref[LAYERS - 1 :, l]
        inner_ref[:, l] = jnp.where(core == 0, last, first)
        outer_ref[:, l] = jnp.where(core == 0, first, last)


def cells_kernel(cells_ref, jac_ref, dissipation_ref, inner_ref, outer_ref, out_ref):
    dissipation = dissipation_ref[...]
    layer = lax.broadcasted_iota(jnp.int32, dissipation.shape, 0)
    core = lax.axis_index("core")
    place = lax.axis_index("y") * 8 + lax.axis_index("z") * 2 + core
    outer = jnp.where((place == 0) | (place == 31), 0.0, outer_ref[...])
    before = jnp.where(core == 0, outer, inner_ref[...])
    after = jnp.where(core == 0, inner_ref[...], outer)
    for g in range(F):
        values = [cells_ref[t, g] for t in range(NT)]
        total = time_sum(values)
        for t in range(NT):
            field = dissipation * values[t]
            at = t * F + g
            lower = jnp.where(layer == 0, before[at : at + 1], pltpu.roll(field, 1, 0))
            upper = jnp.where(layer == LAYERS - 1, after[at : at + 1], pltpu.roll(field, LAYERS - 1, 0))
            out_ref[t, g] = total[t] - (upper - 2.0 * field + lower)
    for t in range(NT):
        field = [cells_ref[t, f] for f in range(F)]
        for g in range(F):
            total = out_ref[t, g]
            for f in range(F):
                total = total + jac_ref[t, f, g].astype(f32) * field[f]
            out_ref[t, g] = total


def in_hbm(*values):
    return tuple(pltpu.with_memory_space_constraint(v, pltpu.HBM) for v in values)


def in_vmem(value):
    return pltpu.with_memory_space_constraint(value, pltpu.VMEM)


def call(kernel, outs, args, flops=0, **more):
    size = sum(math.prod(a.shape) * a.dtype.itemsize for a in (*args, *jax.tree.leaves(outs)))
    return pl.pallas_call(
        kernel,
        out_shape=outs,
        compiler_params=pltpu.CompilerParams(vmem_limit_bytes=24 << 20),
        cost_estimate=pl.CostEstimate(flops=flops, bytes_accessed=size, transcendentals=0),
        **more,
    )(*args)


def shift(value, axis, step):
    size = lax.axis_size(axis)
    return lax.ppermute(value, axis, [(i, (i + step) % size) for i in range(size)])


def body(adjoint_cells, flux_jacobian, dissipation, face_rows, owners, margin_weights, transposed_maps):
    cells = adjoint_cells[0].transpose(1, 2, 0, 3)
    jac = flux_jacobian[0].transpose(1, 2, 3, 0, 4)
    dissipation = dissipation[0]
    faces = face_rows.transpose(1, 2, 0, 3)
    owner = owners.transpose(2, 0, 1)
    margin = margin_weights.transpose(2, 0, 1)
    shape = jax.ShapeDtypeStruct
    hbm = pl.BlockSpec(memory_space=pltpu.HBM)
    vmem = pl.BlockSpec(memory_space=pltpu.VMEM)
    dma = pltpu.SemaphoreType.DMA

    outgoing = call(
        dispatch_kernel,
        pltpu.HBM((SLOTS, WIDTH), bf16),
        in_hbm(faces, owner),
        2 * SLOTS * 2 * ROWS * WIDTH,
        in_specs=[hbm, hbm],
        out_specs=hbm,
        scratch_shapes=[
            pltpu.VMEM(faces.shape, f32),
            pltpu.VMEM(owner.shape, jnp.int32),
            pltpu.VMEM((SLOTS, WIDTH), bf16),
            dma,
            dma,
            dma((PARTS,)),
        ],
    )
    arrived = lax.all_to_all(outgoing.reshape(PEERS, SLOTS // PEERS, WIDTH), SPREAD, 0, 0, tiled=True)

    pieces = []
    for step in STEPS:
        piece = shift(transposed_maps, "z", step) if step else transposed_maps
        pieces += [piece, shift(piece, "core", 1)]

    edge = shape((NT * F, NP), f32)
    lanes = 128
    inner, outer = call(
        edges_kernel,
        (edge, edge),
        in_hbm(cells.reshape(NT * F * LAYERS, NP), dissipation),
        in_specs=[hbm, vmem],
        out_specs=[vmem, vmem],
        scratch_shapes=[pltpu.VMEM((NP // lanes, NT * F * LAYERS, lanes), f32), dma((NP // lanes,))],
    )
    size = lax.axis_size(RADIAL)
    inner, relayed = shift(inner, "core", 1), shift(outer, "core", 1)
    outer = lax.ppermute(relayed, RADIAL, [(i, (i + 2 - 4 * (i % 2)) % size) for i in range(size)])

    weights, time_faces = call(
        weights_kernel,
        (pltpu.HBM((2, ROWS, SLOTS), bf16), pltpu.HBM(faces.shape, f32)),
        in_hbm(faces, owner, margin),
        2 * ROWS * ROWS * SLOTS,
    )

    (outer,) = in_hbm(outer)
    products = call(
        maps_kernel,
        pltpu.HBM((PEERS, SLOTS // PEERS, WIDTH), bf16),
        (in_vmem(arrived), *in_hbm(*pieces), outer),
        2 * SLOTS * F * 8 * FACE * FACE,
        in_specs=[vmem] + [hbm] * 9,
        out_specs=hbm,
        scratch_shapes=[
            pltpu.VMEM((4, 2, 4, FACE, FACE), bf16),
            pltpu.VMEM((4, PEERS, 16, WIDTH), bf16),
            dma((4, 2)),
            dma((4,)),
        ],
    )
    returned = lax.all_to_all(products, SPREAD, 0, 0, tiled=True)

    cell_gradient = call(
        cells_kernel,
        pltpu.HBM(cells.shape, f32),
        in_hbm(cells, jac, dissipation, inner, outer),
        24 * NT * F * LAYERS * NP,
        grid=(NP // lanes,),
        in_specs=[
            pl.BlockSpec((NT, F, LAYERS, lanes), lambda i: (0, 0, 0, i)),
            pl.BlockSpec((NT, F, F, LAYERS, lanes), lambda i: (0, 0, 0, 0, i)),
            pl.BlockSpec((LAYERS, lanes), lambda i: (0, i)),
            pl.BlockSpec((NT * F, lanes), lambda i: (0, i)),
            pl.BlockSpec((NT * F, lanes), lambda i: (0, i)),
        ],
        out_specs=pl.BlockSpec((NT, F, LAYERS, lanes), lambda i: (0, 0, 0, i)),
    )

    face_gradient = call(
        combine_kernel,
        pltpu.HBM(faces.shape, f32),
        (in_vmem(returned.reshape(SLOTS, WIDTH)), *in_hbm(weights, time_faces)),
        4 * ROWS * SLOTS * WIDTH,
        in_specs=[vmem, hbm, hbm],
        out_specs=hbm,
        scratch_shapes=[
            pltpu.VMEM((2, ROWS, SLOTS), bf16),
            pltpu.VMEM(faces.shape, f32),
            pltpu.VMEM(faces.shape, f32),
            dma((3,)),
            dma((3,)),
        ],
    )
    return cell_gradient.transpose(2, 0, 1, 3)[None], face_gradient.transpose(2, 0, 1, 3)


def solution(mesh):
    chips = Mesh(mesh.devices.reshape(4, 4, 4, 2), ("x", "y", "z", "core"))
    every = ("x", "y", "z", "core")
    cells, faces = P("x", RADIAL), P(every)
    return jax.shard_map(
        body,
        mesh=chips,
        in_specs=(cells, cells, cells, faces, faces, faces, faces),
        out_specs=(cells, faces),
        check_vma=False,
    )
```
